128 devices in a mesh: gx: 4 (over x_lo, core), gy: 4 (over z), gz: 8 (over y, x_hi).
Axes of the slice: x: 4 (x_hi: 2, x_lo: 2; x = x_hi * 2 + x_lo), y: 4, z: 4, core: 2. Of those that a mesh axis runs over, the one named last changes fastest.
Arguments:
- volume: float32 [128, 512, 1024], P('gx', 'gy', 'gz'), may hold values from -6 to 6
- offsets: int32 [4, 3], replicated, may hold values from -3 to 3, as said below
Outputs:
- denoised: float32 [128, 512, 1024], P('gx', 'gy', 'gz')
The draws below stay inside these ranges and needn't reach their ends.
Inputs may be any that keep to these rules, and one draw needn't show every extreme that they name: Four distinct offsets; in each the first nonzero component is positive. One offset has first component 3 and a negative third component, another has second component -3, one lies in the plane of the last two dimensions with positive second component, and one lies along the third dimension only; their order is random.
All inputs are finite; a program needn't handle non-finite values.
Results may differ from the reference program's by a relative error of at most 0.00002.
Values sent between devices are 32-bit elements; how exact they have to be, the bound alone decides.
A program may use at most 128 MiB of HBM per device.

```python
import jax
import jax.numpy as jnp
from jax import lax

PAIRS = 4
NX = 128
NY = 512
NZ = 1024


def pick_between(key, low, high):
    return jax.random.randint(key, (), low, high, dtype=jnp.int32)


def draw_offsets(key, part):
    key = jax.random.fold_in(key, 11)
    keys = jax.random.split(key, 8)
    zero = jnp.int32(0)
    first = jnp.stack([jnp.int32(3), pick_between(keys[0], -3, 4), pick_between(keys[1], -3, 0)])
    second = jnp.stack([pick_between(keys[2], 1, 3), jnp.int32(-3), pick_between(keys[3], -3, 4)])
    third = jnp.stack([zero, pick_between(keys[4], 1, 4), pick_between(keys[5], -3, 4)])
    fourth = jnp.stack([zero, zero, pick_between(keys[6], 1, 4)])
    rows = jnp.stack([first, second, third, fourth])
    order = jax.random.permutation(keys[7], 4)
    return rows[order]


def block_levels(key, shape, cuts, least, high):
    def one(axis_at, shards_of):
        heights = jax.random.uniform(jax.random.fold_in(jax.random.fold_in(key, 6), axis_at), (shards_of,), jnp.float32, least / len(cuts), high / len(cuts))
        return jnp.repeat(jnp.exp(heights), shape[axis_at] // shards_of).reshape((-1,) + (1,) * (len(shape) - axis_at - 1))

    factor_of = one(*cuts[0])
    for cut in cuts[1:]:
        factor_of = factor_of * one(*cut)
    return factor_of


def gaussian(own_key, extent, spread, limit, pieces=(), kind=jnp.bfloat16):
    array = jax.random.normal(own_key, extent, jnp.float32) * spread
    if len(pieces) > 0:
        array = block_levels(own_key, extent, pieces, -0.22, 0.18) * array
    return jnp.clip(array, min=-limit, max=limit).astype(kind)


def setup_inputs(seed: int = 0) -> dict:
    key_list = jax.random.split(jax.random.key(seed), 3)
    volume = gaussian(key_list[0], (NX, NY, NZ), 1.0, 6.0, ((0, 4), (1, 4), (2, 8)), jnp.float32)
    offsets = draw_offsets(jax.random.fold_in(key_list[2], 71), 0)
    return {"volume": volume, "offsets": offsets}


def box_sum(field):
    field = field[:-2] + field[1:-1] + field[2:]
    field = field[:, :-2] + field[:, 1:-1] + field[:, 2:]
    return field[:, :, :-2] + field[:, :, 1:-1] + field[:, :, 2:]


def inside_mask(count, shift):
    spots = jnp.arange(count).astype(jnp.int32) + shift
    return (spots >= 0) & (spots < count)


def reference(volume, offsets):
    padded = jnp.pad(volume, 4)
    base = padded[3:-3, 3:-3, 3:-3]
    numer = volume
    denom = jnp.ones_like(volume)
    for k in range(PAIRS):
        first = offsets[k, 0].astype(jnp.int32)
        second = offsets[k, 1].astype(jnp.int32)
        third = offsets[k, 2].astype(jnp.int32)
        partner = lax.dynamic_slice(padded, (3 + first, 3 + second, 3 + third), (NX + 2, NY + 2, NZ + 2))
        diff = base - partner
        dist = box_sum(diff * diff) / 27.0
        inside = inside_mask(NX, first)[:, None, None] & inside_mask(NY, second)[None, :, None] & inside_mask(NZ, third)[None, None, :]
        weight = jnp.where(inside, jnp.exp(-dist * 0.5), jnp.float32(0.0))
        near = partner[1:-1, 1:-1, 1:-1]
        numer = numer + weight * near
        denom = denom + weight
        back_num = lax.dynamic_slice(jnp.pad(weight * volume, 3), (3 - first, 3 - second, 3 - third), (NX, NY, NZ))
        back_den = lax.dynamic_slice(jnp.pad(weight, 3), (3 - first, 3 - second, 3 - third), (NX, NY, NZ))
        numer = numer + back_num
        denom = denom + back_den
    return numer / denom
```

```python
import functools
import math

import jax
import jax.numpy as jnp
from jax import lax
from jax.experimental import pallas as pl
from jax.experimental.pallas import tpu as pltpu
from jax.sharding import PartitionSpec as P

SX, SY, SZ = 32, 128, 128
PAIRS = 4
KAPPA = math.sqrt(math.log2(math.e) / 54.0)
BIG = 16384.0
GROUPS = 9
BLOCK = 5
F32 = jnp.float32
BF16 = jnp.bfloat16
MESH = pl.DeviceIdType.MESH

SIDES = [(dx, dy) for dx in (-1, 0, 1) for dy in (-1, 0, 1) if (dx, dy) != (0, 0)]


def iota(shape, dim):
    return lax.broadcasted_iota(jnp.int32, shape, dim)


def kernel(counts, off, v, out, ext, sh, own, pk_out, pk_in, qh, q2, ql, qr, re, de, eh, el, band, xs, carry, w1, w2,
           send_sem, recv_sem, zsend, zrecv, own_sem):
    nx, ny, nz = counts
    gx, gy, gz = lax.axis_index("gx"), lax.axis_index("gy"), lax.axis_index("gz")

    def have(dx, dy, dz):
        ok = True
        for at, d, n in ((gx, dx, nx), (gy, dy, ny), (gz, dz, nz)):
            if d > 0:
                ok = jnp.logical_and(ok, at + d < n)
            elif d < 0:
                ok = jnp.logical_and(ok, at + d >= 0)
        return ok

    mine = pltpu.make_async_copy(v, ext.at[4:36, 8:136, :], own_sem)
    mine.start()

    barrier = pltpu.get_barrier_semaphore()
    total = jnp.int32(0)
    for dx, dy, dz in [(dx, dy, 0) for dx, dy in SIDES] + [(0, 0, -1), (0, 0, 1)]:
        ok = have(dx, dy, dz)
        total = total + ok.astype(jnp.int32)

        @pl.when(ok)
        def _():
            pl.semaphore_signal(barrier, inc=1, device_id={"gx": gx + dx, "gy": gy + dy, "gz": gz + dz}, device_id_type=MESH)

    pl.semaphore_wait(barrier, total)

    src_x = {1: pl.ds(28, 4), -1: pl.ds(0, 4), 0: pl.ds(0, 32)}
    dst_x = {1: pl.ds(0, 4), -1: pl.ds(36, 4), 0: pl.ds(4, 32)}
    src_y = {1: pl.ds(120, 8), -1: pl.ds(0, 8), 0: pl.ds(0, 128)}
    dst_y = {1: pl.ds(0, 8), -1: pl.ds(136, 8), 0: pl.ds(8, 128)}

    def side_copy(i):
        dx, dy = SIDES[i]
        return pltpu.make_async_remote_copy(
            src_ref=v.at[src_x[dx], src_y[dy], :],
            dst_ref=ext.at[dst_x[dx], dst_y[dy], :],
            send_sem=send_sem.at[i],
            recv_sem=recv_sem.at[i],
            device_id={"gx": gx + dx, "gy": gy + dy},
            device_id_type=MESH,
        )

    for i, (dx, dy) in enumerate(SIDES):

        @pl.when(have(dx, dy, 0))
        def _():
            side_copy(i).start()

        @pl.when(jnp.logical_not(have(-dx, -dy, 0)))
        def _():
            shape = (4 if dx else 32, 8 if dy else 128, 128)
            ext[dst_x[dx], dst_y[dy], :] = jnp.zeros(shape, F32)

    mine.wait()
    for i, (dx, dy) in enumerate(SIDES):

        @pl.when(have(-dx, -dy, 0))
        def _():
            side_copy(i).wait_recv()

    lane = iota((16, 128), 1)
    group = iota((16, 128), 0)
    slot = lane % 8
    low = slot < 4

    def pack_plane(x, _):
        lane8 = iota((8, 128), 1)
        acc = jnp.zeros((8, 128), F32)
        last = jnp.zeros((8, 128), F32)
        for j in range(16):
            here = lane8 // 8 == 15 - j
            turn = (4 + 8 * (15 - j)) % 128
            acc = jnp.where(here, pltpu.roll(ext[x, pl.ds(4 + j, 8, stride=16), :], turn, axis=1), acc)
            if j < 8:
                rows = jnp.broadcast_to(ext[x, pl.ds(132 + j, 1), :], (8, 128))
                last = jnp.where(here, pltpu.roll(rows, turn, axis=1), last)
        own[x, 0:8, :] = acc
        own[x, 8:16, :] = jnp.where(iota((8, 128), 0) == 0, last, 0.0)
        return 0

    lax.fori_loop(0, 40, pack_plane, 0)

    def pack_pair(x, _):
        near, far = own[x], own[x + 20]
        pk_out[0, x] = jnp.where(low, near, pltpu.roll(far, 4, axis=1))
        pk_out[1, x] = jnp.where(low, pltpu.roll(near, 124, axis=1), far)
        return 0

    lax.fori_loop(0, 20, pack_pair, 0)

    def z_copy(i):
        return pltpu.make_async_remote_copy(
            src_ref=pk_out.at[i],
            dst_ref=pk_in.at[i],
            send_sem=zsend.at[i],
            recv_sem=zrecv.at[i],
            device_id={"gz": gz + (1 - 2 * i)},
            device_id_type=MESH,
        )

    for i in range(2):
        d = 1 - 2 * i

        @pl.when(have(0, 0, d))
        def _():
            z_copy(i).start()

        @pl.when(jnp.logical_not(have(0, 0, -d)))
        def _():
            pk_in[i] = jnp.zeros((20, 16, 128), F32)

    def make_band(k, _):
        c = off[k, 2]
        row, col = iota((128, 256), 0), iota((128, 256), 1)
        fwd = col < 128
        spot = jnp.where(fwd, col, col - 128 - c)
        hit = jnp.where(jnp.abs(row - spot) <= 1, -1.0, 0.0)
        s = row % 8
        edge_z = jnp.where(s < 4, s - 4, s + 124)
        edge = jnp.where(jnp.abs(edge_z - spot) <= 1, -1.0, 0.0)
        first = jnp.where(c > 0, 5, 0)
        at = gz * SZ + jnp.where(fwd, col + c, spot)
        beyond = jnp.logical_or(at < 0, at >= nz * SZ)
        edge = jnp.where(s == first, jnp.where(fwd, -BIG, 0.0), edge)
        edge = jnp.where(s == first + 1, jnp.where(fwd, 0.0, -BIG), edge)
        edge = jnp.where(s == first + 2, jnp.where(beyond, -BIG, 0.0), edge)
        hit, edge = hit.astype(BF16), edge.astype(BF16)
        band[k, 0:128, :] = hit
        band[k, 128:256, :] = hit
        band[k, 256:384, :] = edge
        band[k, 384:512, :] = edge
        return 0

    lax.fori_loop(0, PAIRS, make_band, 0)
    xs[...] = jnp.zeros_like(xs)
    re[...] = jnp.zeros_like(re)

    for i in range(2):
        d = 1 - 2 * i

        @pl.when(have(0, 0, -d))
        def _():
            z_copy(i).wait_recv()

    def unpack(x, _):
        left, right = pk_in[0, x], pk_in[1, x]
        for at, from_left, from_right in (
            (x, left, pltpu.roll(right, 4, axis=1)),
            (x + 20, pltpu.roll(left, 124, axis=1), right),
        ):
            mid = own[at]
            halo = jnp.where(low, from_left, from_right) * KAPPA
            qh[at] = halo
            q2[at] = pltpu.roll(halo, 64, axis=1)
            ql[at] = jnp.where(low, from_left, mid) * KAPPA
            qr[at] = jnp.where(low, mid, from_right) * KAPPA
        return 0

    lax.fori_loop(0, 20, unpack, 0)

    def shift_plane(x, _):
        for t in range(18):
            lane8 = iota((8, 128), 1)
            val = ext[x, 8 * t : 8 * t + 8, :] * KAPPA
            halves = []
            if t > 0:
                r0 = 8 * t - 4
                g0, j0 = r0 // 16, r0 % 16
            else:
                g0, j0 = 0, -4
            source = q2 if j0 >= 8 or j0 < 0 else qh
            a = jnp.broadcast_to(source[x, pl.ds(g0, 1), :], (8, 128))
            if j0 + 7 >= 16:
                b = jnp.broadcast_to(source[x, pl.ds(g0 + 1, 1), :], (8, 128))
                a = jnp.where(iota((8, 128), 0) + j0 >= 16, b, a)
            halo = pltpu.roll(a, (8 * (j0 % 8) + 4) % 128, axis=1, stride=8, stride_axis=0)
            sh[3, x, 8 * t : 8 * t + 8, :] = val
            for s in (1, 2, 3):
                sh[3 + s, x, 8 * t : 8 * t + 8, :] = pltpu.roll(jnp.where(lane8 < s, halo, val), 128 - s, axis=1)
                sh[3 - s, x, 8 * t : 8 * t + 8, :] = pltpu.roll(jnp.where(lane8 >= 128 - s, halo, val), s, axis=1)
        return 0

    lax.fori_loop(0, 40, shift_plane, 0)

    def edges(k, _):
        a, b, c = off[k, 0], off[k, 1], off[k, 2]
        turn = lax.rem(128 + 8 * b - c, 128)
        step = jnp.where(b < 0, -1, 1)

        def turned(x, _):
            left = pltpu.roll(ql[x], turn, axis=1)
            right = pltpu.roll(qr[x], turn, axis=1)
            re[x, 8:24, :] = jnp.where(low, left, right)
            return 0

        lax.fori_loop(0, 40, turned, 0)
        row = 15 - lane // 8 + b
        inner = jnp.logical_and(row >= 0, row < 16)

        def squares(x, _):
            same = re[x + a, 8:24, :]
            other = re[x + a, pl.ds(8 + step, 16), :]
            diff = qh[x] - jnp.where(inner, same, other)
            de[x] = diff * diff
            return 0

        lax.fori_loop(0, 37, squares, 0)

        first = jnp.where(c > 0, 5, 0)
        y_at = gy * SY + 16 * group + 15 - lane // 8 - 4
        y_to = y_at + b
        one, zero = jnp.float32(1.0), jnp.float32(0.0)
        out_to = jnp.where(jnp.logical_or(y_to < 0, y_to >= ny * SY), one, zero)
        out_at = jnp.where(jnp.logical_or(y_at < 0, y_at >= ny * SY), one, zero)
        flag_y = jnp.where(slot == first, out_to, jnp.where(slot == first + 1, out_at, one))
        is_flag = jnp.logical_and(slot >= first, slot < first + 3)

        def sums(p, _):
            field = de[p] + de[p + 1] + de[p + 2]
            up = pltpu.roll(field, 8, axis=1)
            up = jnp.where(lane >= 8, up, pltpu.roll(up, 15, axis=0))
            down = pltpu.roll(field, 120, axis=1)
            down = jnp.where(lane < 120, down, pltpu.roll(down, 1, axis=0))
            field = field + up + down
            x_at = gx * SX + p - 3
            x_to = x_at + a
            fx_to = jnp.where(jnp.logical_or(x_to < 0, x_to >= nx * SX), one, zero)
            fx_at = jnp.where(jnp.logical_or(x_at < 0, x_at >= nx * SX), one, zero)
            flag_x = jnp.where(slot == first, fx_to, jnp.where(slot == first + 1, fx_at, zero))
            field = jnp.where(is_flag, jnp.maximum(flag_x, flag_y), field)
            high = field.astype(BF16).astype(F32)
            eh[k, p] = high
            el[k, p] = field - high
            return 0

        lax.fori_loop(0, 35, sums, 0)
        return 0

    lax.fori_loop(0, PAIRS, edges, 0)

    diag = iota((16, 128), 1) // 8 == 15 - iota((16, 128), 0)

    def pair(k, _):
        a, b, c = off[k, 0], off[k, 1], off[k, 2]

        def square(x, t):
            diff = sh[3, x, pl.ds(8 * t + 4, 8), :] - sh[3 + c, x + a, pl.ds(8 * t + 4 + b, 8), :]
            return diff * diff

        for t in range(17):
            d0, d1 = square(0, t), square(1, t)
            carry[0, 8 * t : 8 * t + 8, :] = d0 + d1
            carry[1, 8 * t : 8 * t + 8, :] = d1

        def block(n, _):
            p = n * BLOCK
            for t in range(17):
                rows = slice(8 * t, 8 * t + 8)
                d = [square(p + 2 + i, t) for i in range(5)]
                d01 = d[0] + d[1]
                d23 = d[2] + d[3]
                xs[0, 8 + 8 * t : 16 + 8 * t, :] = carry[0, rows, :] + d[0]
                xs[1, 8 + 8 * t : 16 + 8 * t, :] = carry[1, rows, :] + d01
                xs[2, 8 + 8 * t : 16 + 8 * t, :] = d01 + d[2]
                xs[3, 8 + 8 * t : 16 + 8 * t, :] = d[1] + d23
                xs[4, 8 + 8 * t : 16 + 8 * t, :] = d23 + d[4]
                carry[0, rows, :] = d[3] + d[4]
                carry[1, rows, :] = d[4]
            for i in range(BLOCK):
                left = []
                for g in range(GROUPS):
                    r = 8 + 16 * g
                    field = xs[i, r - 1 : r + 15, :] + xs[i, r : r + 16, :] + xs[i, r + 1 : r + 17, :]
                    high = field.astype(BF16)
                    rest = (field - high.astype(F32)).astype(BF16)
                    e_high = jnp.broadcast_to(eh[k, p + i, pl.ds(g, 1), :], (16, 128)).astype(BF16)
                    e_rest = jnp.broadcast_to(el[k, p + i, pl.ds(g, 1), :], (16, 128)).astype(BF16)
                    zero = jnp.zeros((), BF16)
                    left.append(
                        jnp.concatenate(
                            [high, rest, jnp.where(diag, e_high, zero), jnp.where(diag, e_rest, zero)], axis=1
                        )
                    )
                left = jnp.concatenate(left, axis=0)
                weight = jnp.exp2(jnp.dot(left, band[k], preferred_element_type=F32))
                w1[k, p + i] = weight[0:136, 0:128]
                w2[k, p + i] = weight[0:136, 128:256]
            return 0

        lax.fori_loop(0, 7, block, 0)
        return 0

    lax.fori_loop(0, PAIRS, pair, 0)

    def finish(x, _):
        for t in range(16):
            y = 8 * t
            num = sh[3, x + 4, y + 8 : y + 16, :]
            den = jnp.ones((8, 128), F32)
            for k in range(PAIRS):
                a, b, c = off[k, 0], off[k, 1], off[k, 2]
                near = sh[3 + c, x + 4 + a, pl.ds(y + 8 + b, 8), :]
                back = sh[3 - c, x + 4 - a, pl.ds(y + 8 - b, 8), :]
                fore_w = w1[k, x + 3, y + 4 : y + 12, :]
                back_w = w2[k, x + 3 - a, pl.ds(y + 4 - b, 8), :]
                num = num + fore_w * near + back_w * back
                den = den + fore_w + back_w
            out[x, y : y + 8, :] = num / (den * KAPPA)
        return 0

    lax.fori_loop(0, SX, finish, 0)

    for i, (dx, dy) in enumerate(SIDES):

        @pl.when(have(dx, dy, 0))
        def _():
            side_copy(i).wait_send()

    for i in range(2):

        @pl.when(have(0, 0, 1 - 2 * i))
        def _():
            z_copy(i).wait_send()


def local(counts, volume, offsets):
    return pl.pallas_call(
        functools.partial(kernel, counts),
        out_shape=jax.ShapeDtypeStruct((SX, SY, SZ), F32),
        in_specs=[pl.BlockSpec(memory_space=pltpu.SMEM), pl.BlockSpec(memory_space=pl.ANY)],
        out_specs=pl.BlockSpec(memory_space=pltpu.VMEM),
        scratch_shapes=[
            pltpu.VMEM((40, 144, 128), F32),
            pltpu.VMEM((7, 40, 144, 128), F32),
            pltpu.VMEM((40, 16, 128), F32),
            pltpu.VMEM((2, 20, 16, 128), F32),
            pltpu.VMEM((2, 20, 16, 128), F32),
            pltpu.VMEM((40, 16, 128), F32),
            pltpu.VMEM((40, 16, 128), F32),
            pltpu.VMEM((40, 16, 128), F32),
            pltpu.VMEM((40, 16, 128), F32),
            pltpu.VMEM((40, 32, 128), F32),
            pltpu.VMEM((37, 16, 128), F32),
            pltpu.VMEM((PAIRS, 35, 16, 128), F32),
            pltpu.VMEM((PAIRS, 35, 16, 128), F32),
            pltpu.VMEM((PAIRS, 512, 256), BF16),
            pltpu.VMEM((BLOCK, 168, 128), F32),
            pltpu.VMEM((2, 136, 128), F32),
            pltpu.VMEM((PAIRS, 35, 136, 128), F32),
            pltpu.VMEM((PAIRS, 35, 136, 128), F32),
            pltpu.SemaphoreType.DMA((8,)),
            pltpu.SemaphoreType.DMA((8,)),
            pltpu.SemaphoreType.DMA((2,)),
            pltpu.SemaphoreType.DMA((2,)),
            pltpu.SemaphoreType.DMA,
        ],
        compiler_params=pltpu.CompilerParams(
            collective_id=0, has_side_effects=True, vmem_limit_bytes=62 * 1024 * 1024
        ),
    )(offsets, volume)


def solution(mesh):
    counts = (mesh.shape["gx"], mesh.shape["gy"], mesh.shape["gz"])
    spec = P("gx", "gy", "gz")
    return jax.shard_map(
        functools.partial(local, counts), mesh=mesh, in_specs=(spec, P()), out_specs=spec, check_vma=False
    )
```

```python
import functools
import math

import jax
import jax.numpy as jnp
from jax import lax
from jax.experimental import pallas as pl
from jax.experimental.pallas import tpu as pltpu
from jax.sharding import PartitionSpec as P

SX, SY, SZ = 32, 128, 128
PAIRS = 4
KAPPA = math.sqrt(math.log2(math.e) / 54.0)
BIG = 16384.0
GROUPS = 9
BLOCK = 6
STEPS = 6
TOGETHER = 2
F32 = jnp.float32
BF16 = jnp.bfloat16
MESH = pl.DeviceIdType.MESH

SIDES = [(dx, dy) for dx in (-1, 0, 1) for dy in (-1, 0, 1) if (dx, dy) != (0, 0)]


def iota(shape, dim):
    return lax.broadcasted_iota(jnp.int32, shape, dim)


def kernel(counts, off, v, out, ext, sv, hal, near, own, pk_out, pk_in, qh, ql, qr, re, de, fs, eh, el, band, xa, xb, carry, w1, w2,
           send_sem, recv_sem, zsend, zrecv, own_sem):
    nx, ny, nz = counts
    gx, gy, gz = lax.axis_index("gx"), lax.axis_index("gy"), lax.axis_index("gz")

    def have(dx, dy, dz):
        ok = True
        for at, d, n in ((gx, dx, nx), (gy, dy, ny), (gz, dz, nz)):
            if d > 0:
                ok = jnp.logical_and(ok, at + d < n)
            elif d < 0:
                ok = jnp.logical_and(ok, at + d >= 0)
        return ok

    mine = pltpu.make_async_copy(v, ext.at[4:36, 8:136, :], own_sem)
    mine.start()

    barrier = pltpu.get_barrier_semaphore()
    total = jnp.int32(0)
    for dx, dy, dz in [(dx, dy, 0) for dx, dy in SIDES] + [(0, 0, -1), (0, 0, 1)]:
        ok = have(dx, dy, dz)
        total = total + ok.astype(jnp.int32)

        @pl.when(ok)
        def _():
            pl.semaphore_signal(barrier, inc=1, device_id={"gx": gx + dx, "gy": gy + dy, "gz": gz + dz}, device_id_type=MESH)

    pl.semaphore_wait(barrier, total)

    src_x = {1: pl.ds(28, 4), -1: pl.ds(0, 4), 0: pl.ds(0, 32)}
    dst_x = {1: pl.ds(0, 4), -1: pl.ds(36, 4), 0: pl.ds(4, 32)}
    src_y = {1: pl.ds(120, 8), -1: pl.ds(0, 8), 0: pl.ds(0, 128)}
    dst_y = {1: pl.ds(0, 8), -1: pl.ds(136, 8), 0: pl.ds(8, 128)}

    def side_copy(i):
        dx, dy = SIDES[i]
        return pltpu.make_async_remote_copy(
            src_ref=v.at[src_x[dx], src_y[dy], :],
            dst_ref=ext.at[dst_x[dx], dst_y[dy], :],
            send_sem=send_sem.at[i],
            recv_sem=recv_sem.at[i],
            device_id={"gx": gx + dx, "gy": gy + dy},
            device_id_type=MESH,
        )

    for i, (dx, dy) in enumerate(SIDES):

        @pl.when(have(dx, dy, 0))
        def _():
            side_copy(i).start()

        @pl.when(jnp.logical_not(have(-dx, -dy, 0)))
        def _():
            shape = (4 if dx else 32, 8 if dy else 128, 128)
            ext[dst_x[dx], dst_y[dy], :] = jnp.zeros(shape, F32)

    mine.wait()
    for i, (dx, dy) in enumerate(SIDES):

        @pl.when(have(-dx, -dy, 0))
        def _():
            side_copy(i).wait_recv()

    lane = iota((40, 128), 1)
    slot = lane % 8
    low = slot < 4
    j_of = 15 - lane // 8

    flat = ext.reshape(40 * 144, 128)

    def pack_planes(n, _):
        lane8 = iota((8, 128), 1) // 8
        for i in range(8):
            x = n * 8 + i
            acc = jnp.zeros((8, 128), F32)
            for j in range(16):
                rows = pltpu.roll(ext[x, pl.ds(4 + j, 8, stride=16), :], (124 - 8 * j) % 128, axis=1)
                acc = jnp.where(lane8 == 15 - j, rows, acc)
            own[pl.ds(x, 8, stride=40), :] = acc
        acc = jnp.zeros((8, 128), F32)
        for j in range(8):
            rows = pltpu.roll(flat[pl.ds(n * 8 * 144 + 132 + j, 8, stride=144), :], (124 - 8 * j) % 128, axis=1)
            acc = jnp.where(lane8 == 15 - j, rows, acc)
        own[pl.ds(320 + n * 8, 8), :] = acc
        return 0

    lax.fori_loop(0, 5, pack_planes, 0)

    def mine_at(g):
        return own[40 * g : 40 * g + 40, :]

    for m in range(5):
        this, that = mine_at(m if m < 4 else 8), mine_at(m + 4)
        pk_out[0, m] = jnp.where(low, this, pltpu.roll(that, 4, axis=1))
        pk_out[1, m] = jnp.where(low, pltpu.roll(this, 124, axis=1), that)

    def z_copy(i):
        return pltpu.make_async_remote_copy(
            src_ref=pk_out.at[i],
            dst_ref=pk_in.at[i],
            send_sem=zsend.at[i],
            recv_sem=zrecv.at[i],
            device_id={"gz": gz + (1 - 2 * i)},
            device_id_type=MESH,
        )

    for i in range(2):
        d = 1 - 2 * i

        @pl.when(have(0, 0, d))
        def _():
            z_copy(i).start()

        @pl.when(jnp.logical_not(have(0, 0, -d)))
        def _():
            pk_in[i] = jnp.zeros((5, 40, 128), F32)

    def make_band(k, _):
        c = off[k, 2]
        row, col = iota((128, 256), 0), iota((128, 256), 1)
        fwd = col < 128
        spot = jnp.where(fwd, col, col - 128 - c)
        hit = jnp.where(jnp.abs(row - spot) <= 1, -1.0, 0.0)
        s = row % 8
        edge_z = jnp.where(s < 4, s - 4, s + 124)
        edge = jnp.where(jnp.abs(edge_z - spot) <= 1, -1.0, 0.0)
        first = jnp.where(c > 0, 5, 0)
        at = gz * SZ + jnp.where(fwd, col + c, spot)
        beyond = jnp.logical_or(at < 0, at >= nz * SZ)
        edge = jnp.where(s == first, jnp.where(fwd, -BIG, 0.0), edge)
        edge = jnp.where(s == first + 1, jnp.where(fwd, 0.0, -BIG), edge)
        edge = jnp.where(s == first + 2, jnp.where(beyond, -BIG, 0.0), edge)
        hit, edge = hit.astype(BF16), edge.astype(BF16)
        band[k, 0:128, :] = hit
        band[k, 128:256, :] = hit
        band[k, 256:384, :] = edge
        band[k, 384:512, :] = edge
        return 0

    lax.fori_loop(0, PAIRS, make_band, 0)
    for i in range(BLOCK):
        for xs in (xa, xb):
            xs[i, 0:8, :] = jnp.zeros((8, 128), F32)
            xs[i, 144:168, :] = jnp.zeros((24, 128), F32)
    re[...] = jnp.zeros_like(re)
    sv[40] = jnp.zeros((144, 128), F32)
    hal[40] = jnp.zeros((152, 128), F32)
    fs[:, 0] = jnp.zeros((3, 40, 128), F32)
    fs[:, GROUPS + 1] = jnp.zeros((3, 40, 128), F32)
    de[...] = jnp.zeros_like(de)

    def scale(x, _):
        sv[x] = ext[x] * KAPPA
        return 0

    lax.fori_loop(0, 40, scale, 0)

    row, col = iota((128, 128), 0), iota((128, 128), 1)
    spread_one = jnp.where((row % 8 + 124) % 128 == col, 1.0, 0.0)
    spread_one = spread_one.astype(BF16)
    spread = jnp.concatenate([spread_one, spread_one], axis=0)

    for i in range(2):
        d = 1 - 2 * i

        @pl.when(have(0, 0, -d))
        def _():
            z_copy(i).wait_recv()

    for m in range(5):
        left, right = pk_in[0, m], pk_in[1, m]
        parts = [(m if m < 4 else 8, left, pltpu.roll(right, 4, axis=1))]
        if m < 4:
            parts.append((m + 4, pltpu.roll(left, 124, axis=1), right))
        for g, from_left, from_right in parts:
            mid = mine_at(g)
            qh[g] = jnp.where(low, from_left, from_right) * KAPPA
            ql[g] = jnp.where(low, from_left, mid) * KAPPA
            qr[g] = jnp.where(low, mid, from_right) * KAPPA

    diag = iota((16, 128), 1) // 8 == 15 - iota((16, 128), 0)
    none = jnp.zeros((), BF16)

    def halo_planes(n, _):
        for i in range(4):
            x = n * 4 + i
            left = []
            for g in range(GROUPS):
                field = jnp.broadcast_to(qh[g, pl.ds(x, 1), :], (16, 128))
                high = field.astype(BF16)
                rest = (field - high.astype(F32)).astype(BF16)
                left.append(jnp.concatenate([jnp.where(diag, high, none), jnp.where(diag, rest, none)], axis=1))
            left = jnp.concatenate(left, axis=0)
            hal[x, 4:148, :] = jnp.dot(left, spread, preferred_element_type=F32)
        return 0

    lax.fori_loop(0, 10, halo_planes, 0)

    def edges(k, _):
        a, b, c = off[k, 0], off[k, 1], off[k, 2]
        turn = lax.rem(128 + 8 * b - c, 128)
        step = jnp.where(b < 0, -1, 1)
        for g in range(GROUPS):
            re[g + 1, 0:40, :] = jnp.where(low, pltpu.roll(ql[g], turn, axis=1), pltpu.roll(qr[g], turn, axis=1))
        inner = jnp.logical_and(j_of + b >= 0, j_of + b < 16)
        for g in range(GROUPS):
            partner = jnp.where(inner, re[g + 1, pl.ds(a, 40), :], re[g + 1 + step, pl.ds(a, 40), :])
            diff = qh[g] - partner
            de[g, 0:40, :] = diff * diff
        for g in range(GROUPS):
            field = de[g, 0:40, :] + de[g, 1:41, :] + de[g, 2:42, :]
            fs[0, g + 1] = field
            fs[1, g + 1] = pltpu.roll(field, 8, axis=1)
            fs[2, g + 1] = pltpu.roll(field, 120, axis=1)

        first = jnp.where(c > 0, 5, 0)
        x_at = gx * SX + iota((40, 128), 0) - 3
        x_to = x_at + a
        is_to, is_at, is_one = slot == first, slot == first + 1, slot == first + 2
        off_x_to = jnp.logical_or(x_to < 0, x_to >= nx * SX)
        off_x_at = jnp.logical_or(x_at < 0, x_at >= nx * SX)
        is_flag = jnp.logical_or(jnp.logical_or(is_to, is_at), is_one)
        flag_x = jnp.logical_or(
            jnp.logical_or(jnp.logical_and(is_to, off_x_to), jnp.logical_and(is_at, off_x_at)), is_one
        )
        y_lane = gy * SY - 4 + j_of + jnp.where(is_to, b, 0)
        flag_x = jnp.where(flag_x, 1.0, 0.0)
        for g in range(GROUPS):
            up = jnp.where(lane >= 8, fs[1, g + 1], fs[1, g + 2])
            down = jnp.where(lane < 120, fs[2, g + 1], fs[2, g])
            field = fs[0, g + 1] + up + down
            y = y_lane + 16 * g
            flag = jnp.where(jnp.logical_or(y < 0, y >= ny * SY), 1.0, flag_x)
            field = jnp.where(is_flag, flag, field)
            high = field.astype(BF16).astype(F32)
            eh[k, g] = high
            el[k, g] = field - high
        return 0

    lax.fori_loop(0, PAIRS, edges, 0)

    lane8 = iota((8, 128), 1)

    def shifts(k):
        a, b, c = off[k, 0], off[k, 1], off[k, 2]
        turn = lax.rem(128 - c, 128)
        beyond = jnp.logical_or(lane8 < c, lane8 >= 128 + c)

        def square(x, t):
            rows = pl.ds(b + (8 * t + 4), 8)
            partner = pltpu.roll(jnp.where(beyond, hal[x + a, rows, :], sv[x + a, rows, :]), turn, axis=1)
            near[k, x, 8 * t : 8 * t + 8, :] = partner
            diff = sv[x, 8 * t + 4 : 8 * t + 12, :] - partner
            return diff * diff

        return square

    def begin(k, _):
        square = shifts(k)
        for t in range(17):
            d0, d1 = square(0, t), square(1, t)
            carry[k, 0, 8 * t : 8 * t + 8, :] = d0 + d1
            carry[k, 1, 8 * t : 8 * t + 8, :] = d1
        return 0

    lax.fori_loop(0, PAIRS, begin, 0)

    def field_step(s, xs):
        k = s // STEPS
        p = (s % STEPS) * BLOCK
        square = shifts(k)
        for t in range(17):
            rows = slice(8 * t, 8 * t + 8)
            d = [square(p + 2 + i, t) for i in range(BLOCK)]
            d01, d23, d45 = d[0] + d[1], d[2] + d[3], d[4] + d[5]
            sums = (carry[k, 0, rows, :] + d[0], carry[k, 1, rows, :] + d01, d01 + d[2], d[1] + d23, d23 + d[4], d[3] + d45)
            for i in range(BLOCK):
                xs[i, 8 + 8 * t : 16 + 8 * t, :] = sums[i]
            carry[k, 0, rows, :] = d45
            carry[k, 1, rows, :] = d[5]

    def weight_step(s, xs):
        k = s // STEPS
        p = (s % STEPS) * BLOCK
        for i in range(0, BLOCK, TOGETHER):
            left = []
            for h in range(i, i + TOGETHER):
                for g in range(GROUPS):
                    r = 8 + 16 * g
                    field = xs[h, r - 1 : r + 15, :] + xs[h, r : r + 16, :] + xs[h, r + 1 : r + 17, :]
                    high = field.astype(BF16)
                    rest = (field - high.astype(F32)).astype(BF16)
                    e_high = jnp.broadcast_to(eh[k, g, pl.ds(p + h, 1), :], (16, 128)).astype(BF16)
                    e_rest = jnp.broadcast_to(el[k, g, pl.ds(p + h, 1), :], (16, 128)).astype(BF16)
                    left.append(
                        jnp.concatenate(
                            [high, rest, jnp.where(diag, e_high, none), jnp.where(diag, e_rest, none)], axis=1
                        )
                    )
            left = jnp.concatenate(left, axis=0)
            weight = jnp.exp2(jnp.dot(left, band[k], preferred_element_type=F32))
            for h in range(TOGETHER):
                w1[k, p + i + h] = weight[144 * h : 144 * h + 136, 0:128]
                w2[k, p + i + h] = weight[144 * h : 144 * h + 136, 128:256]

    field_step(0, xa)

    def two_steps(n, _):
        s = 2 * n
        field_step(s + 1, xb)
        weight_step(s, xa)
        field_step(jnp.minimum(s + 2, PAIRS * STEPS - 1), xa)
        weight_step(s + 1, xb)
        return 0

    lax.fori_loop(0, PAIRS * STEPS // 2, two_steps, 0)

    def finish(x, _):
        for t in range(16):
            y = 8 * t
            num = sv[x + 4, y + 8 : y + 16, :]
            den = jnp.ones((8, 128), F32)
            for k in range(PAIRS):
                c = off[k, 2]
                from_x = x - off[k, 0]
                up = jnp.maximum(8 - off[k, 1], 5)
                up_w = jnp.maximum(4 - off[k, 1], 1)
                beyond = jnp.logical_or(lane8 < 0 - c, lane8 >= 128 - c)
                rows = pl.ds(up + y, 8)
                back = jnp.where(beyond, hal[from_x + 4, rows, :], sv[from_x + 4, rows, :])
                back = pltpu.roll(back, lax.rem(128 + c, 128), axis=1)
                fore_w = w1[k, x + 3, y + 4 : y + 12, :]
                back_w = w2[k, from_x + 3, pl.ds(up_w + y, 8), :]
                num = num + fore_w * near[k, x + 4, y + 4 : y + 12, :] + back_w * back
                den = den + fore_w + back_w
            out[x, y : y + 8, :] = num / (den * KAPPA)
        return 0

    lax.fori_loop(0, SX, finish, 0)

    for i, (dx, dy) in enumerate(SIDES):

        @pl.when(have(dx, dy, 0))
        def _():
            side_copy(i).wait_send()

    for i in range(2):

        @pl.when(have(0, 0, 1 - 2 * i))
        def _():
            z_copy(i).wait_send()


def local(counts, volume, offsets):
    return pl.pallas_call(
        functools.partial(kernel, counts),
        out_shape=jax.ShapeDtypeStruct((SX, SY, SZ), F32),
        in_specs=[pl.BlockSpec(memory_space=pltpu.SMEM), pl.BlockSpec(memory_space=pl.ANY)],
        out_specs=pl.BlockSpec(memory_space=pltpu.VMEM),
        scratch_shapes=[
            pltpu.VMEM((40, 144, 128), F32),
            pltpu.VMEM((41, 144, 128), F32),
            pltpu.VMEM((41, 152, 128), F32),
            pltpu.VMEM((PAIRS, 38, 136, 128), F32),
            pltpu.VMEM((GROUPS * 40, 128), F32),
            pltpu.VMEM((2, 5, 40, 128), F32),
            pltpu.VMEM((2, 5, 40, 128), F32),
            pltpu.VMEM((GROUPS, 40, 128), F32),
            pltpu.VMEM((GROUPS, 40, 128), F32),
            pltpu.VMEM((GROUPS, 40, 128), F32),
            pltpu.VMEM((GROUPS + 2, 48, 128), F32),
            pltpu.VMEM((GROUPS, 48, 128), F32),
            pltpu.VMEM((3, GROUPS + 2, 40, 128), F32),
            pltpu.VMEM((PAIRS, GROUPS, 40, 128), F32),
            pltpu.VMEM((PAIRS, GROUPS, 40, 128), F32),
            pltpu.VMEM((PAIRS, 512, 256), BF16),
            pltpu.VMEM((BLOCK, 168, 128), F32),
            pltpu.VMEM((BLOCK, 168, 128), F32),
            pltpu.VMEM((PAIRS, 2, 136, 128), F32),
            pltpu.VMEM((PAIRS, 36, 136, 128), F32),
            pltpu.VMEM((PAIRS, 36, 136, 128), F32),
            pltpu.SemaphoreType.DMA((8,)),
            pltpu.SemaphoreType.DMA((8,)),
            pltpu.SemaphoreType.DMA((2,)),
            pltpu.SemaphoreType.DMA((2,)),
            pltpu.SemaphoreType.DMA,
        ],
        compiler_params=pltpu.CompilerParams(
            collective_id=0, has_side_effects=True, vmem_limit_bytes=62 * 1024 * 1024
        ),
    )(offsets, volume)


def solution(mesh):
    counts = (mesh.shape["gx"], mesh.shape["gy"], mesh.shape["gz"])
    spec = P("gx", "gy", "gz")
    return jax.shard_map(
        functools.partial(local, counts), mesh=mesh, in_specs=(spec, P()), out_specs=spec, check_vma=False
    )
```

```python
import functools
import math

import jax
import jax.numpy as jnp
from jax import lax
from jax.experimental import pallas as pl
from jax.experimental.pallas import tpu as pltpu
from jax.sharding import PartitionSpec as P

SX, SY, SZ = 32, 128, 128
PAIRS = 4
KAPPA = math.sqrt(math.log2(math.e) / 54.0)
BIG = 16384.0
GROUPS = 9
BLOCK = 6
TOGETHER = 3
F32 = jnp.float32
BF16 = jnp.bfloat16
MESH = pl.DeviceIdType.MESH

SIDES = [(dx, dy) for dx in (-1, 0, 1) for dy in (-1, 0, 1) if (dx, dy) != (0, 0)]


FRIENDS = [(dx, dy, 0) for dx, dy in SIDES] + [(0, dy, dz) for dy in (-1, 0, 1) for dz in (-1, 1)]


def iota(shape, dim):
    return lax.broadcasted_iota(jnp.int32, shape, dim)


def kernel(counts, off, v, out, ext, sv, hal, near, own, pk_out, pk_in, yz_out, yz_in, xe_out, xe_in, qh, qm, re, de, fs,
           eh, el, band, xa, xb, carry, w1, w2, t2, done, send_sem, recv_sem, own_sem, out_sem):
    nx, ny, nz = counts
    gx, gy, gz = lax.axis_index("gx"), lax.axis_index("gy"), lax.axis_index("gz")

    def have(dx, dy, dz):
        ok = True
        for at, d, n in ((gx, dx, nx), (gy, dy, ny), (gz, dz, nz)):
            if d > 0:
                ok = jnp.logical_and(ok, at + d < n)
            elif d < 0:
                ok = jnp.logical_and(ok, at + d >= 0)
        return ok

    mine = pltpu.make_async_copy(v, ext.at[4:36, 8:136, :], own_sem)
    mine.start()

    barrier = pltpu.get_barrier_semaphore()
    total = jnp.int32(0)
    for dx, dy, dz in FRIENDS:
        ok = have(dx, dy, dz)
        total = total + ok.astype(jnp.int32)

        @pl.when(ok)
        def _():
            pl.semaphore_signal(barrier, inc=1, device_id={"gx": gx + dx, "gy": gy + dy, "gz": gz + dz}, device_id_type=MESH)

    src_x = {1: pl.ds(28, 4), -1: pl.ds(0, 4), 0: pl.ds(0, 32)}
    dst_x = {1: pl.ds(0, 4), -1: pl.ds(36, 4), 0: pl.ds(4, 32)}
    src_y = {1: pl.ds(120, 8), -1: pl.ds(0, 8), 0: pl.ds(0, 128)}
    dst_y = {1: pl.ds(0, 8), -1: pl.ds(136, 8), 0: pl.ds(8, 128)}

    def copy(way, src, dst, n):
        return pltpu.make_async_remote_copy(
            src_ref=src,
            dst_ref=dst,
            send_sem=send_sem.at[n],
            recv_sem=recv_sem.at[n],
            device_id={"gx": gx + way[0], "gy": gy + way[1], "gz": gz + way[2]},
            device_id_type=MESH,
        )

    side = {}
    for i, (dx, dy) in enumerate(SIDES):
        place = ext.at[dst_x[dx], dst_y[dy], :]
        side[dx, dy] = ((dx, dy, 0), v.at[src_x[dx], src_y[dy], :], place, i)
    across = [((0, 0, 1 - 2 * i), pk_out.at[i], pk_in.at[i], 8 + i) for i in range(2)]
    corner = [
        ((0, 1 - 2 * j, 1 - 2 * i), yz_out.at[j], yz_in.at[i, j], 10 + 2 * i + j) for i in range(2) for j in range(2)
    ]
    ends = [((1 - 2 * i, 0, 0), xe_out.at[i], xe_in.at[i], 14 + i) for i in range(2)]
    slabs = [side[key] for key in side if key[0] != 0]
    strips = [side[key] for key in side if key[0] == 0]

    def start(item):
        @pl.when(have(*item[0]))
        def _():
            copy(*item).start()

    def clear(item):
        way, place = item[0], item[2]

        @pl.when(jnp.logical_not(have(-way[0], -way[1], -way[2])))
        def _():
            place[...] = jnp.zeros(place.shape, F32)

    def arrive(item):
        way = item[0]

        @pl.when(have(-way[0], -way[1], -way[2]))
        def _():
            copy(*item).wait_recv()

    def leave(item):
        @pl.when(have(*item[0]))
        def _():
            copy(*item).wait_send()

    mine.wait()

    lane = iota((40, 128), 1)
    slot = lane % 8
    low = slot < 4
    j_of = 15 - lane // 8
    lane32 = iota((32, 128), 1)
    low32 = lane32 % 8 < 4
    lane8 = iota((8, 128), 1)
    low8 = lane8 % 8 < 4

    def pack_planes(n, _):
        for i in range(8):
            x = n * 8 + i
            acc = jnp.zeros((8, 128), F32)
            for j in range(16):
                first = 4 + j if j >= 4 else 20 + j
                rows = pltpu.roll(ext[x + 4, pl.ds(first, 8, stride=16), :], (124 - 8 * j) % 128, axis=1)
                acc = jnp.where(lane8 // 8 == 15 - j, rows, acc)
            own[pl.ds(x, 8, stride=32), :] = acc
        return 0

    lax.fori_loop(0, 4, pack_planes, 0)

    def mine_at(i):
        return own[32 * i : 32 * i + 32, :]

    for m in range(4):
        this, that = mine_at(m), mine_at(m + 4)
        pk_out[0, m] = jnp.where(low32, this, pltpu.roll(that, 4, axis=1))
        pk_out[1, m] = jnp.where(low32, pltpu.roll(this, 124, axis=1), that)
    for j, (block, lanes) in enumerate(((7, 96), (0, 64))):
        acc = jnp.zeros((8, 128), F32)
        for q in range(4):
            rows = own[32 * block + 8 * q : 32 * block + 8 * q + 8, :]
            acc = jnp.where(lane8 // 32 == q, pltpu.roll(rows, (32 * q - lanes) % 128, axis=1), acc)
        yz_out[j] = acc
    pl.semaphore_wait(barrier, total)
    for item in corner + across + strips + slabs:
        start(item)

    for item in strips + across + corner + slabs + ends:
        clear(item)

    def make_band(k, _):
        c = off[k, 2]
        row, col = iota((128, 256), 0), iota((128, 256), 1)
        fwd = col < 128
        spot = jnp.where(fwd, col, col - 128 - c)
        hit = jnp.where(jnp.abs(row - spot) <= 1, -1.0, 0.0)
        s = row % 8
        edge_z = jnp.where(s < 4, s - 4, s + 124)
        edge = jnp.where(jnp.abs(edge_z - spot) <= 1, -1.0, 0.0)
        first = jnp.where(c > 0, 5, 0)
        at = gz * SZ + jnp.where(fwd, col + c, spot)
        beyond = jnp.logical_or(at < 0, at >= nz * SZ)
        edge = jnp.where(s == first, jnp.where(fwd, -BIG, 0.0), edge)
        edge = jnp.where(s == first + 1, jnp.where(fwd, 0.0, -BIG), edge)
        edge = jnp.where(s == first + 2, jnp.where(beyond, -BIG, 0.0), edge)
        hit, edge = hit.astype(BF16), edge.astype(BF16)
        band[k, 0:128, :] = hit
        band[k, 128:256, :] = hit
        band[k, 256:384, :] = edge
        band[k, 384:512, :] = edge
        return 0

    lax.fori_loop(0, PAIRS, make_band, 0)
    for i in range(BLOCK):
        for xs in (xa, xb):
            xs[i, 0:8, :] = jnp.zeros((8, 128), F32)
            xs[i, 144:168, :] = jnp.zeros((24, 128), F32)
    re[...] = jnp.zeros_like(re)
    de[...] = jnp.zeros_like(de)
    for x in (0, 1, 2, 3, 36, 37, 38, 39, 40):
        sv[x] = jnp.zeros((144, 128), F32)
        hal[x] = jnp.zeros((152, 128), F32)
    for g in range(GROUPS):
        qh[g] = jnp.zeros((40, 128), F32)
        qm[g] = jnp.zeros((40, 128), F32)
    fs[:, 0] = jnp.zeros((3, 40, 128), F32)
    fs[:, GROUPS + 1] = jnp.zeros((3, 40, 128), F32)
    carry[...] = jnp.zeros_like(carry)

    row, col = iota((128, 128), 0), iota((128, 128), 1)
    spread_one = jnp.where((row % 8 + 124) % 128 == col, 1.0, 0.0).astype(BF16)
    spread = jnp.concatenate([spread_one, spread_one], axis=0)

    def scale(n, _):
        for i in range(4):
            x = 4 + 4 * n + i
            sv[x, 8:136, :] = ext[x, 8:136, :] * KAPPA
        return 0

    lax.fori_loop(0, 8, scale, 0)
    for item in strips:
        arrive(item)
    for x in range(4, 36):
        sv[x, 0:8, :] = ext[x, 0:8, :] * KAPPA
        sv[x, 136:144, :] = ext[x, 136:144, :] * KAPPA

    flat = ext.reshape(40 * 144, 128)
    beyond_low, beyond_high = [], []
    for q in range(4):
        acc_low, acc_high = jnp.zeros((8, 128), F32), jnp.zeros((8, 128), F32)
        base = (4 + 8 * q) * 144
        for j in range(4):
            rows = pltpu.roll(flat[pl.ds(base + 4 + j, 8, stride=144), :], (124 - 8 * j) % 128, axis=1)
            acc_low = jnp.where(lane8 // 8 == 15 - j, rows, acc_low)
            rows = pltpu.roll(flat[pl.ds(base + 136 + j, 8, stride=144), :], (92 - 8 * j) % 128, axis=1)
            acc_high = jnp.where(lane8 // 8 == 11 - j, rows, acc_high)
        beyond_low.append(acc_low)
        beyond_high.append(acc_high)
    mids = [jnp.concatenate(beyond_low, axis=0)] + [mine_at(i) for i in range(8)] + [jnp.concatenate(beyond_high, axis=0)]
    for g in range(GROUPS):
        qm[g, 4:36, :] = jnp.where(lane32 < 96, mids[g + 1], mids[g]) * KAPPA

    for item in across + corner:
        arrive(item)
    halos = [None] * 10
    for j, (block, lanes) in enumerate(((0, 96), (9, 64))):
        both = jnp.where(low8, yz_in[0, j], yz_in[1, j])
        parts = [pltpu.roll(both, (lanes - 32 * q) % 128, axis=1) for q in range(4)]
        halos[block] = jnp.concatenate(parts, axis=0)
    for m in range(4):
        left, right = pk_in[0, m], pk_in[1, m]
        halos[1 + m] = jnp.where(low32, left, pltpu.roll(right, 4, axis=1))
        halos[5 + m] = jnp.where(low32, pltpu.roll(left, 124, axis=1), right)
    for g in range(GROUPS):
        qh[g, 4:36, :] = jnp.where(lane32 < 96, halos[g + 1], halos[g]) * KAPPA
    for g in range(GROUPS):
        for i, first in enumerate((32, 4)):
            xe_out[i, g, 0:4, :] = qh[g, first : first + 4, :]
            xe_out[i, g, 4:8, :] = qm[g, first : first + 4, :]
    for item in ends:
        start(item)

    diag = iota((16, 128), 1) // 8 == 15 - iota((16, 128), 0)
    none = jnp.zeros((), BF16)

    def halo_planes(planes):
        left = []
        for x in planes:
            for g in range(GROUPS):
                field = jnp.broadcast_to(qh[g, pl.ds(x, 1), :], (16, 128))
                high = field.astype(BF16)
                rest = (field - high.astype(F32)).astype(BF16)
                left.append(jnp.concatenate([jnp.where(diag, high, none), jnp.where(diag, rest, none)], axis=1))
        left = jnp.concatenate(left, axis=0)
        spot = jnp.dot(left, spread, preferred_element_type=F32)
        for i, x in enumerate(planes):
            hal[x, 4:148, :] = spot[144 * i : 144 * i + 144]

    def edges(spans_d, spans_p, planes):
        def one(k, _):
            edge_pair(k, spans_d, spans_p)
            halo_planes(planes(k))
            return 0

        lax.fori_loop(0, PAIRS, one, 0)

    def edge_pair(k, spans_d, spans_p):
        a, b, c = off[k, 0], off[k, 1], off[k, 2]
        turn = lax.rem(128 + 8 * b - c, 128)
        step = jnp.where(b < 0, -1, 1)
        same = low == (slot - c < 4)
        for g in range(GROUPS):
            re[g + 1, 0:40, :] = pltpu.roll(jnp.where(same, qh[g], qm[g]), turn, axis=1)

        def lanes_of(n):
            lane_n = iota((n, 128), 1)
            return lane_n, lane_n % 8, 15 - lane_n // 8

        for first, n in spans_d:
            _, _, j_n = lanes_of(n)
            inner = jnp.logical_and(j_n + b >= 0, j_n + b < 16)
            for g in range(GROUPS):
                rows = pl.ds(a + first, n)
                diff = qh[g, first : first + n, :] - jnp.where(inner, re[g + 1, rows, :], re[g + 1 + step, rows, :])
                de[g, first : first + n, :] = diff * diff
        flag0 = jnp.where(c > 0, 5, 0)
        for first, n in spans_p:
            lane_n, slot_n, j_n = lanes_of(n)
            for g in range(GROUPS):
                field = de[g, first : first + n, :] + de[g, first + 1 : first + n + 1, :] + de[g, first + 2 : first + n + 2, :]
                fs[0, g + 1, first : first + n, :] = field
                fs[1, g + 1, first : first + n, :] = pltpu.roll(field, 8, axis=1)
                fs[2, g + 1, first : first + n, :] = pltpu.roll(field, 120, axis=1)
            x_at = gx * SX + iota((n, 128), 0) + (first - 3)
            is_to, is_at, is_one = slot_n == flag0, slot_n == flag0 + 1, slot_n == flag0 + 2
            x = x_at + jnp.where(is_to, a, 0)
            off_x = jnp.logical_or(is_one, jnp.logical_or(x < 0, x >= nx * SX))
            flag_x = jnp.where(off_x, 1.0, 0.0)
            is_flag = jnp.logical_and(slot_n >= flag0, slot_n < flag0 + 3)
            y_lane = gy * SY - 4 + j_n + jnp.where(is_to, b, 0)
            for g in range(GROUPS):
                rows = slice(first, first + n)
                up = jnp.where(lane_n >= 8, fs[1, g + 1, rows, :], fs[1, g + 2, rows, :])
                down = jnp.where(lane_n < 120, fs[2, g + 1, rows, :], fs[2, g, rows, :])
                field = fs[0, g + 1, rows, :] + up + down
                flag = flag_x
                if g in (0, GROUPS - 1):
                    y = y_lane + 16 * g
                    flag = jnp.where(jnp.logical_or(y < 0, y >= ny * SY), 1.0, flag_x)
                field = jnp.where(is_flag, flag, field)
                high = field.astype(BF16).astype(F32)
                eh[k, g, rows, :] = high
                el[k, g, rows, :] = field - high

    edges([(0, 32)], [(0, 32)], lambda k: [4 + 8 * k + i for i in range(8)])


    def shifts(k):
        a, b, c = off[k, 0], off[k, 1], off[k, 2]
        turn = lax.rem(128 - c, 128)
        beyond = jnp.logical_or(lane8 < c, lane8 >= 128 + c)

        def square(x, t):
            rows = pl.ds(b + (8 * t + 4), 8)
            partner = pltpu.roll(jnp.where(beyond, hal[x + a, rows, :], sv[x + a, rows, :]), turn, axis=1)
            near[k, x, 8 * t : 8 * t + 8, :] = partner
            diff = sv[x, 8 * t + 4 : 8 * t + 12, :] - partner
            return diff * diff

        return square

    def begin(p, slot):
        def one(k, _):
            square = shifts(k)
            for t in range(17):
                d0, d1 = square(p, t), square(p + 1, t)
                carry[slot, k, 0, 8 * t : 8 * t + 8, :] = d0 + d1
                carry[slot, k, 1, 8 * t : 8 * t + 8, :] = d1
            return 0

        lax.fori_loop(0, PAIRS, one, 0)

    def field_step(k, n, slot, xs):
        p = n * BLOCK
        square = shifts(k)
        for t in range(17):
            rows = slice(8 * t, 8 * t + 8)
            d = [square(p + 2 + i, t) for i in range(BLOCK)]
            d01, d23, d45 = d[0] + d[1], d[2] + d[3], d[4] + d[5]
            sums = (carry[slot, k, 0, rows, :] + d[0], carry[slot, k, 1, rows, :] + d01, d01 + d[2], d[1] + d23, d23 + d[4], d[3] + d45)
            for i in range(BLOCK):
                xs[i, 8 + 8 * t : 16 + 8 * t, :] = sums[i]
            carry[slot, k, 0, rows, :] = d45
            carry[slot, k, 1, rows, :] = d[5]

    def weight_step(k, n, xs):
        p = n * BLOCK
        c = off[k, 2]
        beyond = jnp.logical_or(lane8 < 0 - c, lane8 >= 128 - c)
        turn = lax.rem(128 + c, 128)
        for i in range(0, BLOCK, TOGETHER):
            left = []
            for h in range(i, i + TOGETHER):
                for g in range(GROUPS):
                    r = 8 + 16 * g
                    field = xs[h, r - 1 : r + 15, :] + xs[h, r : r + 16, :] + xs[h, r + 1 : r + 17, :]
                    high = field.astype(BF16)
                    rest = (field - high.astype(F32)).astype(BF16)
                    e_high = jnp.broadcast_to(eh[k, g, pl.ds(p + h, 1), :], (16, 128)).astype(BF16)
                    e_rest = jnp.broadcast_to(el[k, g, pl.ds(p + h, 1), :], (16, 128)).astype(BF16)
                    left.append(
                        jnp.concatenate(
                            [high, rest, jnp.where(diag, e_high, none), jnp.where(diag, e_rest, none)], axis=1
                        )
                    )
            left = jnp.concatenate(left, axis=0)
            weight = jnp.exp2(jnp.dot(left, band[k], preferred_element_type=F32))
            for h in range(TOGETHER):
                w1[k, p + i + h] = weight[144 * h : 144 * h + 136, 0:128]
                w2[k, p + i + h] = weight[144 * h : 144 * h + 136, 128:256]
                for t in range(17):
                    rows, at = slice(8 * t, 8 * t + 8), slice(8 * t + 4, 8 * t + 12)
                    x = p + i + h + 1
                    back = pltpu.roll(jnp.where(beyond, hal[x, at, :], sv[x, at, :]), turn, axis=1)
                    t2[k, p + i + h, rows, :] = back * weight[144 * h + 8 * t : 144 * h + 8 * t + 8, 128:256]

    def run(steps, place):
        def field(s, xs):
            k, n, slot = place(jnp.minimum(s, steps - 1))
            field_step(k, n, jnp.where(s < steps, slot, 2), xs)

        def weigh(s, xs):
            k, n, _ = place(s)
            weight_step(k, n, xs)

        field(jnp.int32(0), xa)

        def two_steps(i, _):
            s = 2 * i
            field(s + 1, xb)
            weigh(s, xa)
            field(s + 2, xa)
            weigh(s + 1, xb)
            return 0

        lax.fori_loop(0, steps // 2, two_steps, 0)

    begin(BLOCK, 0)
    run(PAIRS * 4, lambda s: (s // 4, 1 + s % 4, 0))

    for item in slabs + ends:
        arrive(item)
    for x in (0, 1, 2, 3, 36, 37, 38, 39):
        sv[x] = ext[x] * KAPPA
    for g in range(GROUPS):
        for i, first in enumerate((0, 36)):
            qh[g, first : first + 4, :] = xe_in[i, g, 0:4, :]
            qm[g, first : first + 4, :] = xe_in[i, g, 4:8, :]

    edges([(0, 16), (24, 16)], [(0, 8), (24, 16)], lambda k: [k, k + 36])
    begin(0, 1)
    run(PAIRS * 2, lambda s: (s // 2, 5 * (s % 2), 1 - s % 2))

    w2f, t2f = w2.reshape(PAIRS * 36 * 136, 128), t2.reshape(PAIRS * 36 * 136, 128)
    froms = [
        jnp.maximum((k * 36 + 3 - off[k, 0]) * 136 + 4 - off[k, 1], 1) for k in range(PAIRS)
    ]

    def finish(n, _):
        for x in (2 * n, 2 * n + 1):
            bases = [froms[k] + x * 136 for k in range(PAIRS)]
            for t in range(16):
                y = 8 * t
                num = sv[x + 4, y + 8 : y + 16, :]
                den = jnp.ones((8, 128), F32)
                for k in range(PAIRS):
                    rows = pl.ds(bases[k] + y, 8)
                    fore_w = w1[k, x + 3, y + 4 : y + 12, :]
                    num = num + (fore_w * near[k, x + 4, y + 4 : y + 12, :] + t2f[rows, :])
                    den = den + (fore_w + w2f[rows, :])
                done[x, y : y + 8, :] = num / (den * KAPPA)
            pltpu.make_async_copy(done.at[x], out.at[x], out_sem).start()
        return 0

    lax.fori_loop(0, SX // 2, finish, 0)
    pltpu.make_async_copy(done, out, out_sem).wait()
    for item in strips + across + corner + slabs + ends:
        leave(item)


PARTS = 4


def hand_over(src, dst, held, sems):
    n = SX // PARTS
    spans = [pl.ds(n * i, n) for i in range(PARTS)]
    ins = [pltpu.make_async_copy(src.at[span], held.at[span], sems.at[0, i]) for i, span in enumerate(spans)]
    outs = [pltpu.make_async_copy(held.at[span], dst.at[span], sems.at[1, i]) for i, span in enumerate(spans)]
    for item in ins:
        item.start()
    for first, then in zip(ins, outs):
        first.wait()
        then.start()
    for item in outs:
        item.wait()


def local(counts, volume, offsets):
    result = pl.pallas_call(
        functools.partial(kernel, counts),
        out_shape=jax.ShapeDtypeStruct((SX, SY, SZ), F32),
        in_specs=[pl.BlockSpec(memory_space=pltpu.SMEM), pl.BlockSpec(memory_space=pl.ANY)],
        out_specs=pl.BlockSpec(memory_space=pl.ANY),
        scratch_shapes=[
            pltpu.VMEM((40, 144, 128), F32),
            pltpu.VMEM((41, 144, 128), F32),
            pltpu.VMEM((41, 152, 128), F32),
            pltpu.VMEM((PAIRS, 38, 136, 128), F32),
            pltpu.VMEM((8 * 32, 128), F32),
            pltpu.VMEM((2, 4, 32, 128), F32),
            pltpu.VMEM((2, 4, 32, 128), F32),
            pltpu.VMEM((2, 8, 128), F32),
            pltpu.VMEM((2, 2, 8, 128), F32),
            pltpu.VMEM((2, GROUPS, 8, 128), F32),
            pltpu.VMEM((2, GROUPS, 8, 128), F32),
            pltpu.VMEM((GROUPS, 40, 128), F32),
            pltpu.VMEM((GROUPS, 40, 128), F32),
            pltpu.VMEM((GROUPS + 2, 48, 128), F32),
            pltpu.VMEM((GROUPS, 48, 128), F32),
            pltpu.VMEM((3, GROUPS + 2, 40, 128), F32),
            pltpu.VMEM((PAIRS, GROUPS, 40, 128), F32),
            pltpu.VMEM((PAIRS, GROUPS, 40, 128), F32),
            pltpu.VMEM((PAIRS, 512, 256), BF16),
            pltpu.VMEM((BLOCK, 168, 128), F32),
            pltpu.VMEM((BLOCK, 168, 128), F32),
            pltpu.VMEM((3, PAIRS, 2, 136, 128), F32),
            pltpu.VMEM((PAIRS, 36, 136, 128), F32),
            pltpu.VMEM((PAIRS, 36, 136, 128), F32),
            pltpu.VMEM((PAIRS, 36, 136, 128), F32),
            pltpu.VMEM((SX, SY, SZ), F32),
            pltpu.SemaphoreType.DMA((16,)),
            pltpu.SemaphoreType.DMA((16,)),
            pltpu.SemaphoreType.DMA,
            pltpu.SemaphoreType.DMA,
        ],
        compiler_params=pltpu.CompilerParams(
            collective_id=0, has_side_effects=True, vmem_limit_bytes=62 * 1024 * 1024
        ),
    )(offsets, volume)
    return pl.pallas_call(
        hand_over,
        out_shape=jax.ShapeDtypeStruct((SX, SY, SZ), F32),
        in_specs=[pl.BlockSpec(memory_space=pl.ANY)],
        out_specs=pl.BlockSpec(memory_space=pl.ANY),
        scratch_shapes=[pltpu.VMEM((SX, SY, SZ), F32), pltpu.SemaphoreType.DMA((2, PARTS))],
    )(result)


def solution(mesh):
    counts = (mesh.shape["gx"], mesh.shape["gy"], mesh.shape["gz"])
    spec = P("gx", "gy", "gz")
    return jax.shard_map(
        functools.partial(local, counts), mesh=mesh, in_specs=(spec, P()), out_specs=spec, check_vma=False
    )
```

```python
import functools
import math

import jax
import jax.numpy as jnp
from jax import lax
from jax.experimental import pallas as pl
from jax.experimental.pallas import tpu as pltpu
from jax.sharding import PartitionSpec as P

SX, SY, SZ = 32, 128, 128
PAIRS = 4
KAPPA = math.sqrt(math.log2(math.e) / 54.0)
BIG = 16384.0
GROUPS = 9
BLOCK = 6
TOGETHER = 3
F32 = jnp.float32
BF16 = jnp.bfloat16
MESH = pl.DeviceIdType.MESH

SIDES = [(dx, dy) for dx in (-1, 0, 1) for dy in (-1, 0, 1) if (dx, dy) != (0, 0)]


FRIENDS = [(dx, dy, 0) for dx, dy in SIDES] + [(0, dy, dz) for dy in (-1, 0, 1) for dz in (-1, 1)]


def iota(shape, dim):
    return lax.broadcasted_iota(jnp.int32, shape, dim)


def kernel(counts, off, v, out, ext, sv, hal, near, own, pk_out, pk_in, yz_out, yz_in, xe_out, xe_in, qh, qm, re, de, fs,
           eh, el, band, xa, xb, carry, w1, w2, t2, done, send_sem, recv_sem, own_sem, out_sem):
    nx, ny, nz = counts
    gx, gy, gz = lax.axis_index("gx"), lax.axis_index("gy"), lax.axis_index("gz")

    def have(dx, dy, dz):
        ok = True
        for at, d, n in ((gx, dx, nx), (gy, dy, ny), (gz, dz, nz)):
            if d > 0:
                ok = jnp.logical_and(ok, at + d < n)
            elif d < 0:
                ok = jnp.logical_and(ok, at + d >= 0)
        return ok

    mine = [
        pltpu.make_async_copy(v.at[pl.ds(8 * n, 8)], ext.at[pl.ds(4 + 8 * n, 8), pl.ds(8, 128), :], own_sem.at[n])
        for n in range(4)
    ]
    for item in mine:
        item.start()

    barrier = pltpu.get_barrier_semaphore()
    total = jnp.int32(0)
    for dx, dy, dz in FRIENDS:
        ok = have(dx, dy, dz)
        total = total + ok.astype(jnp.int32)

        @pl.when(ok)
        def _():
            pl.semaphore_signal(barrier, inc=1, device_id={"gx": gx + dx, "gy": gy + dy, "gz": gz + dz}, device_id_type=MESH)

    src_x = {1: pl.ds(28, 4), -1: pl.ds(0, 4), 0: pl.ds(0, 32)}
    dst_x = {1: pl.ds(0, 4), -1: pl.ds(36, 4), 0: pl.ds(4, 32)}
    src_y = {1: pl.ds(124, 4), -1: pl.ds(0, 4), 0: pl.ds(0, 128)}
    dst_y = {1: pl.ds(4, 4), -1: pl.ds(136, 4), 0: pl.ds(8, 128)}

    def copy(way, src, dst, n):
        return pltpu.make_async_remote_copy(
            src_ref=src,
            dst_ref=dst,
            send_sem=send_sem.at[n],
            recv_sem=recv_sem.at[n],
            device_id={"gx": gx + way[0], "gy": gy + way[1], "gz": gz + way[2]},
            device_id_type=MESH,
        )

    side = {}
    for i, (dx, dy) in enumerate(SIDES):
        place = ext.at[dst_x[dx], dst_y[dy], :]
        side[dx, dy] = ((dx, dy, 0), v.at[src_x[dx], src_y[dy], :], place, i)
    across = [((0, 0, 1 - 2 * i), pk_out.at[i], pk_in.at[i], 8 + i) for i in range(2)]
    corner = [
        ((0, 1 - 2 * j, 1 - 2 * i), yz_out.at[j], yz_in.at[i, j], 10 + 2 * i + j) for i in range(2) for j in range(2)
    ]
    ends = [((1 - 2 * i, 0, 0), xe_out.at[i], xe_in.at[i], 14 + i) for i in range(2)]
    slabs = [side[key] for key in side if key[0] != 0]
    strips = [side[key] for key in side if key[0] == 0]

    def start(item):
        @pl.when(have(*item[0]))
        def _():
            copy(*item).start()

    def clear(item):
        way, place = item[0], item[2]

        @pl.when(jnp.logical_not(have(-way[0], -way[1], -way[2])))
        def _():
            place[...] = jnp.zeros(place.shape, F32)

    def arrive(item):
        way = item[0]

        @pl.when(have(-way[0], -way[1], -way[2]))
        def _():
            copy(*item).wait_recv()

    def leave(item):
        @pl.when(have(*item[0]))
        def _():
            copy(*item).wait_send()


    lane = iota((40, 128), 1)
    slot = lane % 8
    low = slot < 4
    j_of = 15 - lane // 8
    lane32 = iota((32, 128), 1)
    low32 = lane32 % 8 < 4
    lane8 = iota((8, 128), 1)
    low8 = lane8 % 8 < 4

    for n in range(4):
        mine[n].wait()
        for i in range(8):
            x = n * 8 + i
            acc = jnp.zeros((8, 128), F32)
            for j in range(16):
                first = 4 + j if j >= 4 else 20 + j
                rows = pltpu.roll(ext[x + 4, pl.ds(first, 8, stride=16), :], (124 - 8 * j) % 128, axis=1)
                acc = jnp.where(lane8 // 8 == 15 - j, rows, acc)
            own[pl.ds(x, 8, stride=32), :] = acc

    def mine_at(i):
        return own[32 * i : 32 * i + 32, :]

    for m in range(4):
        this, that = mine_at(m), mine_at(m + 4)
        pk_out[0, m] = jnp.where(low32, this, pltpu.roll(that, 4, axis=1))
        pk_out[1, m] = jnp.where(low32, pltpu.roll(this, 124, axis=1), that)
    for j, (block, lanes) in enumerate(((7, 96), (0, 64))):
        acc = jnp.zeros((8, 128), F32)
        for q in range(4):
            rows = own[32 * block + 8 * q : 32 * block + 8 * q + 8, :]
            acc = jnp.where(lane8 // 32 == q, pltpu.roll(rows, (32 * q - lanes) % 128, axis=1), acc)
        yz_out[j] = acc
    pl.semaphore_wait(barrier, total)
    for item in corner + across + strips + slabs:
        start(item)

    for item in strips + across + corner + slabs + ends:
        clear(item)

    def make_band(k, _):
        c = off[k, 2]
        row, col = iota((128, 256), 0), iota((128, 256), 1)
        fwd = col < 128
        spot = jnp.where(fwd, col, col - 128 - c)
        hit = jnp.where(jnp.abs(row - spot) <= 1, -1.0, 0.0)
        s = row % 8
        edge_z = jnp.where(s < 4, s - 4, s + 124)
        edge = jnp.where(jnp.abs(edge_z - spot) <= 1, -1.0, 0.0)
        first = jnp.where(c > 0, 5, 0)
        at = gz * SZ + jnp.where(fwd, col + c, spot)
        beyond = jnp.logical_or(at < 0, at >= nz * SZ)
        edge = jnp.where(s == first, jnp.where(fwd, -BIG, 0.0), edge)
        edge = jnp.where(s == first + 1, jnp.where(fwd, 0.0, -BIG), edge)
        edge = jnp.where(s == first + 2, jnp.where(beyond, -BIG, 0.0), edge)
        hit, edge = hit.astype(BF16), edge.astype(BF16)
        band[k, 0:128, :] = hit
        band[k, 128:256, :] = hit
        band[k, 256:384, :] = edge
        band[k, 384:512, :] = edge
        return 0

    lax.fori_loop(0, PAIRS, make_band, 0)
    for i in range(BLOCK):
        for xs in (xa, xb):
            xs[i, 0:8, :] = jnp.zeros((8, 128), F32)
            xs[i, 144:168, :] = jnp.zeros((24, 128), F32)
    re[...] = jnp.zeros_like(re)
    de[...] = jnp.zeros_like(de)
    for x in (0, 1, 2, 3, 36, 37, 38, 39, 40):
        sv[x] = jnp.zeros((144, 128), F32)
        hal[x] = jnp.zeros((152, 128), F32)
    for g in range(GROUPS):
        qh[g] = jnp.zeros((40, 128), F32)
        qm[g] = jnp.zeros((40, 128), F32)
    fs[:, 0] = jnp.zeros((3, 40, 128), F32)
    fs[:, GROUPS + 1] = jnp.zeros((3, 40, 128), F32)
    carry[...] = jnp.zeros_like(carry)

    row, col = iota((128, 128), 0), iota((128, 128), 1)
    spread_one = jnp.where((row % 8 + 124) % 128 == col, 1.0, 0.0).astype(BF16)
    spread = jnp.concatenate([spread_one, spread_one], axis=0)

    def scale(n, _):
        for i in range(4):
            x = 4 + 4 * n + i
            sv[x, 8:136, :] = ext[x, 8:136, :] * KAPPA
        return 0

    lax.fori_loop(0, 8, scale, 0)
    for item in strips:
        arrive(item)
    for x in range(4, 36):
        sv[x, 0:8, :] = ext[x, 0:8, :] * KAPPA
        sv[x, 136:144, :] = ext[x, 136:144, :] * KAPPA

    flat = ext.reshape(40 * 144, 128)
    beyond_low, beyond_high = [], []
    for q in range(4):
        acc_low, acc_high = jnp.zeros((8, 128), F32), jnp.zeros((8, 128), F32)
        base = (4 + 8 * q) * 144
        for j in range(4):
            rows = pltpu.roll(flat[pl.ds(base + 4 + j, 8, stride=144), :], (124 - 8 * j) % 128, axis=1)
            acc_low = jnp.where(lane8 // 8 == 15 - j, rows, acc_low)
            rows = pltpu.roll(flat[pl.ds(base + 136 + j, 8, stride=144), :], (92 - 8 * j) % 128, axis=1)
            acc_high = jnp.where(lane8 // 8 == 11 - j, rows, acc_high)
        beyond_low.append(acc_low)
        beyond_high.append(acc_high)
    mids = [jnp.concatenate(beyond_low, axis=0)] + [mine_at(i) for i in range(8)] + [jnp.concatenate(beyond_high, axis=0)]
    for g in range(GROUPS):
        qm[g, 4:36, :] = jnp.where(lane32 < 96, mids[g + 1], mids[g]) * KAPPA

    for item in across + corner:
        arrive(item)
    halos = [None] * 10
    for j, (block, lanes) in enumerate(((0, 96), (9, 64))):
        both = jnp.where(low8, yz_in[0, j], yz_in[1, j])
        parts = [pltpu.roll(both, (lanes - 32 * q) % 128, axis=1) for q in range(4)]
        halos[block] = jnp.concatenate(parts, axis=0)
    for m in range(4):
        left, right = pk_in[0, m], pk_in[1, m]
        halos[1 + m] = jnp.where(low32, left, pltpu.roll(right, 4, axis=1))
        halos[5 + m] = jnp.where(low32, pltpu.roll(left, 124, axis=1), right)
    for g in range(GROUPS):
        qh[g, 4:36, :] = jnp.where(lane32 < 96, halos[g + 1], halos[g]) * KAPPA
    for g in range(GROUPS):
        for i, first in enumerate((32, 4)):
            xe_out[i, g, 0:4, :] = qh[g, first : first + 4, :]
            xe_out[i, g, 4:8, :] = qm[g, first : first + 4, :]
    for item in ends:
        start(item)

    diag = iota((16, 128), 1) // 8 == 15 - iota((16, 128), 0)
    none = jnp.zeros((), BF16)

    def halo_planes(planes):
        left = []
        for x in planes:
            for g in range(GROUPS):
                field = jnp.broadcast_to(qh[g, pl.ds(x, 1), :], (16, 128))
                high = field.astype(BF16)
                rest = (field - high.astype(F32)).astype(BF16)
                left.append(jnp.concatenate([jnp.where(diag, high, none), jnp.where(diag, rest, none)], axis=1))
        left = jnp.concatenate(left, axis=0)
        spot = jnp.dot(left, spread, preferred_element_type=F32)
        for i, x in enumerate(planes):
            hal[x, 4:148, :] = spot[144 * i : 144 * i + 144]

    def edges(spans_d, spans_p, planes):
        def one(k, _):
            edge_pair(k, spans_d, spans_p)
            halo_planes(planes(k))
            return 0

        lax.fori_loop(0, PAIRS, one, 0)

    def edge_pair(k, spans_d, spans_p):
        a, b, c = off[k, 0], off[k, 1], off[k, 2]
        turn = lax.rem(128 + 8 * b - c, 128)
        step = jnp.where(b < 0, -1, 1)
        same = low == (slot - c < 4)
        for g in range(GROUPS):
            re[g + 1, 0:40, :] = pltpu.roll(jnp.where(same, qh[g], qm[g]), turn, axis=1)

        def lanes_of(n):
            lane_n = iota((n, 128), 1)
            return lane_n, lane_n % 8, 15 - lane_n // 8

        for first, n in spans_d:
            _, _, j_n = lanes_of(n)
            inner = jnp.logical_and(j_n + b >= 0, j_n + b < 16)
            for g in range(GROUPS):
                rows = pl.ds(a + first, n)
                diff = qh[g, first : first + n, :] - jnp.where(inner, re[g + 1, rows, :], re[g + 1 + step, rows, :])
                de[g, first : first + n, :] = diff * diff
        flag0 = jnp.where(c > 0, 5, 0)
        for first, n in spans_p:
            lane_n, slot_n, j_n = lanes_of(n)
            for g in range(GROUPS):
                field = de[g, first : first + n, :] + de[g, first + 1 : first + n + 1, :] + de[g, first + 2 : first + n + 2, :]
                fs[0, g + 1, first : first + n, :] = field
                fs[1, g + 1, first : first + n, :] = pltpu.roll(field, 8, axis=1)
                fs[2, g + 1, first : first + n, :] = pltpu.roll(field, 120, axis=1)
            x_at = gx * SX + iota((n, 128), 0) + (first - 3)
            is_to, is_at, is_one = slot_n == flag0, slot_n == flag0 + 1, slot_n == flag0 + 2
            x = x_at + jnp.where(is_to, a, 0)
            off_x = jnp.logical_or(is_one, jnp.logical_or(x < 0, x >= nx * SX))
            flag_x = jnp.where(off_x, 1.0, 0.0)
            is_flag = jnp.logical_and(slot_n >= flag0, slot_n < flag0 + 3)
            y_lane = gy * SY - 4 + j_n + jnp.where(is_to, b, 0)
            for g in range(GROUPS):
                rows = slice(first, first + n)
                up = jnp.where(lane_n >= 8, fs[1, g + 1, rows, :], fs[1, g + 2, rows, :])
                down = jnp.where(lane_n < 120, fs[2, g + 1, rows, :], fs[2, g, rows, :])
                field = fs[0, g + 1, rows, :] + up + down
                flag = flag_x
                if g in (0, GROUPS - 1):
                    y = y_lane + 16 * g
                    flag = jnp.where(jnp.logical_or(y < 0, y >= ny * SY), 1.0, flag_x)
                field = jnp.where(is_flag, flag, field)
                high = field.astype(BF16).astype(F32)
                eh[k, g, rows, :] = high
                el[k, g, rows, :] = field - high

    edges([(0, 32)], [(0, 32)], lambda k: [4 + 8 * k + i for i in range(8)])


    def shifts(k):
        a, b, c = off[k, 0], off[k, 1], off[k, 2]
        turn = lax.rem(128 - c, 128)
        beyond = jnp.logical_or(lane8 < c, lane8 >= 128 + c)

        def square(x, t):
            rows = pl.ds(b + (8 * t + 4), 8)
            partner = pltpu.roll(jnp.where(beyond, hal[x + a, rows, :], sv[x + a, rows, :]), turn, axis=1)
            near[k, x, 8 * t : 8 * t + 8, :] = partner
            diff = sv[x, 8 * t + 4 : 8 * t + 12, :] - partner
            return diff * diff

        return square

    def begin(p, slot):
        def one(k, _):
            square = shifts(k)
            for t in range(17):
                d0, d1 = square(p, t), square(p + 1, t)
                carry[slot, k, 0, 8 * t : 8 * t + 8, :] = d0 + d1
                carry[slot, k, 1, 8 * t : 8 * t + 8, :] = d1
            return 0

        lax.fori_loop(0, PAIRS, one, 0)

    def field_step(k, n, slot, xs):
        p = n * BLOCK
        square = shifts(k)
        for t in range(17):
            rows = slice(8 * t, 8 * t + 8)
            d = [square(p + 2 + i, t) for i in range(BLOCK)]
            d01, d23, d45 = d[0] + d[1], d[2] + d[3], d[4] + d[5]
            sums = (carry[slot, k, 0, rows, :] + d[0], carry[slot, k, 1, rows, :] + d01, d01 + d[2], d[1] + d23, d23 + d[4], d[3] + d45)
            for i in range(BLOCK):
                xs[i, 8 + 8 * t : 16 + 8 * t, :] = sums[i]
            carry[slot, k, 0, rows, :] = d45
            carry[slot, k, 1, rows, :] = d[5]

    def weight_step(k, n, xs):
        p = n * BLOCK
        c = off[k, 2]
        beyond = jnp.logical_or(lane8 < 0 - c, lane8 >= 128 - c)
        turn = lax.rem(128 + c, 128)
        for i in range(0, BLOCK, TOGETHER):
            left = []
            for h in range(i, i + TOGETHER):
                for g in range(GROUPS):
                    r = 8 + 16 * g
                    field = xs[h, r - 1 : r + 15, :] + xs[h, r : r + 16, :] + xs[h, r + 1 : r + 17, :]
                    high = field.astype(BF16)
                    rest = (field - high.astype(F32)).astype(BF16)
                    e_high = jnp.broadcast_to(eh[k, g, pl.ds(p + h, 1), :], (16, 128)).astype(BF16)
                    e_rest = jnp.broadcast_to(el[k, g, pl.ds(p + h, 1), :], (16, 128)).astype(BF16)
                    left.append(
                        jnp.concatenate(
                            [high, rest, jnp.where(diag, e_high, none), jnp.where(diag, e_rest, none)], axis=1
                        )
                    )
            left = jnp.concatenate(left, axis=0)
            weight = jnp.exp2(jnp.dot(left, band[k], preferred_element_type=F32))
            for h in range(TOGETHER):
                w1[k, p + i + h] = weight[144 * h : 144 * h + 136, 0:128]
                w2[k, p + i + h] = weight[144 * h : 144 * h + 136, 128:256]
                for t in range(17):
                    rows, at = slice(8 * t, 8 * t + 8), slice(8 * t + 4, 8 * t + 12)
                    x = p + i + h + 1
                    back = pltpu.roll(jnp.where(beyond, hal[x, at, :], sv[x, at, :]), turn, axis=1)
                    t2[k, p + i + h, rows, :] = back * weight[144 * h + 8 * t : 144 * h + 8 * t + 8, 128:256]

    def run(steps, place):
        def field(s, xs):
            k, n, slot = place(jnp.minimum(s, steps - 1))
            field_step(k, n, jnp.where(s < steps, slot, 2), xs)

        def weigh(s, xs):
            k, n, _ = place(s)
            weight_step(k, n, xs)

        field(jnp.int32(0), xa)

        def two_steps(i, _):
            s = 4 * i
            field(s + 1, xb)
            weigh(s, xa)
            field(s + 2, xa)
            weigh(s + 1, xb)
            field(s + 3, xb)
            weigh(s + 2, xa)
            field(s + 4, xa)
            weigh(s + 3, xb)
            return 0

        lax.fori_loop(0, steps // 4, two_steps, 0)

    begin(BLOCK, 0)
    run(PAIRS * 4, lambda s: (s // 4, 1 + s % 4, 0))

    for item in slabs + ends:
        arrive(item)
    for x in (0, 1, 2, 3, 36, 37, 38, 39):
        sv[x] = ext[x] * KAPPA
    for g in range(GROUPS):
        for i, first in enumerate((0, 36)):
            qh[g, first : first + 4, :] = xe_in[i, g, 0:4, :]
            qm[g, first : first + 4, :] = xe_in[i, g, 4:8, :]

    edges([(0, 16), (24, 16)], [(0, 8), (24, 16)], lambda k: [k, k + 36])
    begin(0, 1)
    run(PAIRS * 2, lambda s: (s // 2, 5 * (s % 2), 1 - s % 2))

    w2f, t2f = w2.reshape(PAIRS * 36 * 136, 128), t2.reshape(PAIRS * 36 * 136, 128)
    froms = [
        jnp.maximum((k * 36 + 3 - off[k, 0]) * 136 + 4 - off[k, 1], 1) for k in range(PAIRS)
    ]

    def finish(n, _):
        for x in (2 * n, 2 * n + 1):
            bases = [froms[k] + x * 136 for k in range(PAIRS)]
            for t in range(16):
                y = 8 * t
                num = sv[x + 4, y + 8 : y + 16, :]
                den = jnp.ones((8, 128), F32)
                for k in range(PAIRS):
                    rows = pl.ds(bases[k] + y, 8)
                    fore_w = w1[k, x + 3, y + 4 : y + 12, :]
                    num = num + (fore_w * near[k, x + 4, y + 4 : y + 12, :] + t2f[rows, :])
                    den = den + (fore_w + w2f[rows, :])
                done[x, y : y + 8, :] = num / (den * KAPPA)
            pltpu.make_async_copy(done.at[x], out.at[x], out_sem).start()
        return 0

    lax.fori_loop(0, SX // 2, finish, 0)
    pltpu.make_async_copy(done, out, out_sem).wait()
    for item in strips + across + corner + slabs + ends:
        leave(item)


PARTS = 4


def hand_over(src, dst, held, sems):
    n = SX // PARTS
    spans = [pl.ds(n * i, n) for i in range(PARTS)]
    ins = [pltpu.make_async_copy(src.at[span], held.at[span], sems.at[0, i]) for i, span in enumerate(spans)]
    outs = [pltpu.make_async_copy(held.at[span], dst.at[span], sems.at[1, i]) for i, span in enumerate(spans)]
    for item in ins:
        item.start()
    for first, then in zip(ins, outs):
        first.wait()
        then.start()
    for item in outs:
        item.wait()


def local(counts, volume, offsets):
    result = pl.pallas_call(
        functools.partial(kernel, counts),
        out_shape=jax.ShapeDtypeStruct((SX, SY, SZ), F32),
        in_specs=[pl.BlockSpec(memory_space=pltpu.SMEM), pl.BlockSpec(memory_space=pl.ANY)],
        out_specs=pl.BlockSpec(memory_space=pl.ANY),
        scratch_shapes=[
            pltpu.VMEM((40, 144, 128), F32),
            pltpu.VMEM((41, 144, 128), F32),
            pltpu.VMEM((41, 152, 128), F32),
            pltpu.VMEM((PAIRS, 38, 136, 128), F32),
            pltpu.VMEM((8 * 32, 128), F32),
            pltpu.VMEM((2, 4, 32, 128), F32),
            pltpu.VMEM((2, 4, 32, 128), F32),
            pltpu.VMEM((2, 8, 128), F32),
            pltpu.VMEM((2, 2, 8, 128), F32),
            pltpu.VMEM((2, GROUPS, 8, 128), F32),
            pltpu.VMEM((2, GROUPS, 8, 128), F32),
            pltpu.VMEM((GROUPS, 40, 128), F32),
            pltpu.VMEM((GROUPS, 40, 128), F32),
            pltpu.VMEM((GROUPS + 2, 48, 128), F32),
            pltpu.VMEM((GROUPS, 48, 128), F32),
            pltpu.VMEM((3, GROUPS + 2, 40, 128), F32),
            pltpu.VMEM((PAIRS, GROUPS, 40, 128), F32),
            pltpu.VMEM((PAIRS, GROUPS, 40, 128), F32),
            pltpu.VMEM((PAIRS, 512, 256), BF16),
            pltpu.VMEM((BLOCK, 168, 128), F32),
            pltpu.VMEM((BLOCK, 168, 128), F32),
            pltpu.VMEM((3, PAIRS, 2, 136, 128), F32),
            pltpu.VMEM((PAIRS, 36, 136, 128), F32),
            pltpu.VMEM((PAIRS, 36, 136, 128), F32),
            pltpu.VMEM((PAIRS, 36, 136, 128), F32),
            pltpu.VMEM((SX, SY, SZ), F32),
            pltpu.SemaphoreType.DMA((16,)),
            pltpu.SemaphoreType.DMA((16,)),
            pltpu.SemaphoreType.DMA((4,)),
            pltpu.SemaphoreType.DMA,
        ],
        compiler_params=pltpu.CompilerParams(
            collective_id=0, has_side_effects=True, vmem_limit_bytes=62 * 1024 * 1024
        ),
    )(offsets, volume)
    return pl.pallas_call(
        hand_over,
        out_shape=jax.ShapeDtypeStruct((SX, SY, SZ), F32),
        in_specs=[pl.BlockSpec(memory_space=pl.ANY)],
        out_specs=pl.BlockSpec(memory_space=pl.ANY),
        scratch_shapes=[pltpu.VMEM((SX, SY, SZ), F32), pltpu.SemaphoreType.DMA((2, PARTS))],
    )(result)


def solution(mesh):
    counts = (mesh.shape["gx"], mesh.shape["gy"], mesh.shape["gz"])
    spec = P("gx", "gy", "gz")
    return jax.shard_map(
        functools.partial(local, counts), mesh=mesh, in_specs=(spec, P()), out_specs=spec, check_vma=False
    )
```

```python
import functools
import math

import jax
import jax.numpy as jnp
from jax import lax
from jax.experimental import pallas as pl
from jax.experimental.pallas import tpu as pltpu
from jax.sharding import PartitionSpec as P

SX, SY, SZ = 32, 128, 128
PAIRS = 4
KAPPA = math.sqrt(math.log2(math.e) / 54.0)
BIG = 16384.0
GROUPS = 9
BLOCK = 6
TOGETHER = 3
F32 = jnp.float32
BF16 = jnp.bfloat16
MESH = pl.DeviceIdType.MESH

SIDES = [(dx, dy) for dx in (-1, 0, 1) for dy in (-1, 0, 1) if (dx, dy) != (0, 0)]


FRIENDS = [(dx, dy, 0) for dx, dy in SIDES] + [(0, dy, dz) for dy in (-1, 0, 1) for dz in (-1, 1)]


def iota(shape, dim):
    return lax.broadcasted_iota(jnp.int32, shape, dim)


def kernel(counts, off, v, out, ext, sv, hal, near, own, pk_out, pk_in, yz_out, yz_in, xe_out, xe_in, qh, qm, re, de, fs,
           eh, el, band, xa, xb, carry, w1, w2, t2, done, send_sem, recv_sem, own_sem, out_sem):
    nx, ny, nz = counts
    gx, gy, gz = lax.axis_index("gx"), lax.axis_index("gy"), lax.axis_index("gz")

    def have(dx, dy, dz):
        ok = True
        for at, d, n in ((gx, dx, nx), (gy, dy, ny), (gz, dz, nz)):
            if d > 0:
                ok = jnp.logical_and(ok, at + d < n)
            elif d < 0:
                ok = jnp.logical_and(ok, at + d >= 0)
        return ok

    mine = [
        pltpu.make_async_copy(v.at[pl.ds(8 * n, 8)], ext.at[pl.ds(4 + 8 * n, 8), pl.ds(8, 128), :], own_sem.at[n])
        for n in range(4)
    ]
    for item in mine:
        item.start()

    barrier = pltpu.get_barrier_semaphore()
    total = jnp.int32(0)
    for dx, dy, dz in FRIENDS:
        ok = have(dx, dy, dz)
        total = total + ok.astype(jnp.int32)

        @pl.when(ok)
        def _():
            pl.semaphore_signal(barrier, inc=1, device_id={"gx": gx + dx, "gy": gy + dy, "gz": gz + dz}, device_id_type=MESH)

    src_x = {1: pl.ds(28, 4), -1: pl.ds(0, 4), 0: pl.ds(0, 32)}
    dst_x = {1: pl.ds(0, 4), -1: pl.ds(36, 4), 0: pl.ds(4, 32)}
    src_y = {1: pl.ds(124, 4), -1: pl.ds(0, 4), 0: pl.ds(0, 128)}
    dst_y = {1: pl.ds(4, 4), -1: pl.ds(136, 4), 0: pl.ds(8, 128)}

    def copy(way, src, dst, n):
        return pltpu.make_async_remote_copy(
            src_ref=src,
            dst_ref=dst,
            send_sem=send_sem.at[n],
            recv_sem=recv_sem.at[n],
            device_id={"gx": gx + way[0], "gy": gy + way[1], "gz": gz + way[2]},
            device_id_type=MESH,
        )

    side = {}
    for i, (dx, dy) in enumerate(SIDES):
        place = ext.at[dst_x[dx], dst_y[dy], :]
        side[dx, dy] = ((dx, dy, 0), v.at[src_x[dx], src_y[dy], :], place, i)
    across = [((0, 0, 1 - 2 * i), pk_out.at[i], pk_in.at[i], 8 + i) for i in range(2)]
    corner = [
        ((0, 1 - 2 * j, 1 - 2 * i), yz_out.at[j], yz_in.at[i, j], 10 + 2 * i + j) for i in range(2) for j in range(2)
    ]
    ends = [((1 - 2 * i, 0, 0), xe_out.at[i], xe_in.at[i], 14 + i) for i in range(2)]
    slabs = [side[key] for key in side if key[0] != 0]
    strips = [side[key] for key in side if key[0] == 0]

    def start(item):
        @pl.when(have(*item[0]))
        def _():
            copy(*item).start()

    def clear(item):
        way, place = item[0], item[2]

        @pl.when(jnp.logical_not(have(-way[0], -way[1], -way[2])))
        def _():
            place[...] = jnp.zeros(place.shape, F32)

    def arrive(item):
        way = item[0]

        @pl.when(have(-way[0], -way[1], -way[2]))
        def _():
            copy(*item).wait_recv()

    def leave(item):
        @pl.when(have(*item[0]))
        def _():
            copy(*item).wait_send()


    lane = iota((40, 128), 1)
    slot = lane % 8
    low = slot < 4
    j_of = 15 - lane // 8
    lane32 = iota((32, 128), 1)
    low32 = lane32 % 8 < 4
    lane8 = iota((8, 128), 1)
    low8 = lane8 % 8 < 4

    for n in range(4):
        mine[n].wait()
        for i in range(8):
            x = n * 8 + i
            acc = jnp.zeros((8, 128), F32)
            for j in range(16):
                first = 4 + j if j >= 4 else 20 + j
                rows = pltpu.roll(ext[x + 4, pl.ds(first, 8, stride=16), :], (124 - 8 * j) % 128, axis=1)
                acc = jnp.where(lane8 // 8 == 15 - j, rows, acc)
            own[pl.ds(x, 8, stride=32), :] = acc

    def mine_at(i):
        return own[32 * i : 32 * i + 32, :]

    for m in range(4):
        this, that = mine_at(m), mine_at(m + 4)
        pk_out[0, m] = jnp.where(low32, this, pltpu.roll(that, 4, axis=1))
        pk_out[1, m] = jnp.where(low32, pltpu.roll(this, 124, axis=1), that)
    for j, (block, lanes) in enumerate(((7, 96), (0, 64))):
        acc = jnp.zeros((8, 128), F32)
        for q in range(4):
            rows = own[32 * block + 8 * q : 32 * block + 8 * q + 8, :]
            acc = jnp.where(lane8 // 32 == q, pltpu.roll(rows, (32 * q - lanes) % 128, axis=1), acc)
        yz_out[j] = acc
    pl.semaphore_wait(barrier, total)
    for item in corner + across + strips + slabs:
        start(item)

    for item in strips + across + corner + slabs + ends:
        clear(item)

    def make_band(k, _):
        c = off[k, 2]
        row, col = iota((128, 256), 0), iota((128, 256), 1)
        fwd = col < 128
        spot = jnp.where(fwd, col, col - 128 - c)
        hit = jnp.where(jnp.abs(row - spot) <= 1, -1.0, 0.0)
        s = row % 8
        edge_z = jnp.where(s < 4, s - 4, s + 124)
        edge = jnp.where(jnp.abs(edge_z - spot) <= 1, -1.0, 0.0)
        first = jnp.where(c > 0, 5, 0)
        at = gz * SZ + jnp.where(fwd, col + c, spot)
        beyond = jnp.logical_or(at < 0, at >= nz * SZ)
        edge = jnp.where(s == first, jnp.where(fwd, -BIG, 0.0), edge)
        edge = jnp.where(s == first + 1, jnp.where(fwd, 0.0, -BIG), edge)
        edge = jnp.where(s == first + 2, jnp.where(beyond, -BIG, 0.0), edge)
        hit, edge = hit.astype(BF16), edge.astype(BF16)
        band[k, 0:128, :] = hit
        band[k, 128:256, :] = hit
        band[k, 256:384, :] = edge
        band[k, 384:512, :] = edge
        return 0

    lax.fori_loop(0, PAIRS, make_band, 0)
    for i in range(BLOCK):
        for xs in (xa, xb):
            xs[i, 0:8, :] = jnp.zeros((8, 128), F32)
            xs[i, 144:168, :] = jnp.zeros((24, 128), F32)
    re[...] = jnp.zeros_like(re)
    de[...] = jnp.zeros_like(de)
    for x in (0, 1, 2, 3, 36, 37, 38, 39, 40):
        sv[x] = jnp.zeros((144, 128), F32)
        hal[x] = jnp.zeros((152, 128), F32)
    for g in range(GROUPS):
        qh[g] = jnp.zeros((40, 128), F32)
        qm[g] = jnp.zeros((40, 128), F32)
    fs[:, 0] = jnp.zeros((3, 40, 128), F32)
    fs[:, GROUPS + 1] = jnp.zeros((3, 40, 128), F32)
    carry[...] = jnp.zeros_like(carry)

    row, col = iota((128, 128), 0), iota((128, 128), 1)
    spread_one = jnp.where((row % 8 + 124) % 128 == col, 1.0, 0.0).astype(BF16)
    spread = jnp.concatenate([spread_one, spread_one], axis=0)

    def scale(n, _):
        for i in range(4):
            x = 4 + 4 * n + i
            sv[x, 8:136, :] = ext[x, 8:136, :] * KAPPA
        return 0

    lax.fori_loop(0, 8, scale, 0)
    for item in strips:
        arrive(item)
    for x in range(4, 36):
        sv[x, 0:8, :] = ext[x, 0:8, :] * KAPPA
        sv[x, 136:144, :] = ext[x, 136:144, :] * KAPPA

    flat = ext.reshape(40 * 144, 128)
    beyond_low, beyond_high = [], []
    for q in range(4):
        acc_low, acc_high = jnp.zeros((8, 128), F32), jnp.zeros((8, 128), F32)
        base = (4 + 8 * q) * 144
        for j in range(4):
            rows = pltpu.roll(flat[pl.ds(base + 4 + j, 8, stride=144), :], (124 - 8 * j) % 128, axis=1)
            acc_low = jnp.where(lane8 // 8 == 15 - j, rows, acc_low)
            rows = pltpu.roll(flat[pl.ds(base + 136 + j, 8, stride=144), :], (92 - 8 * j) % 128, axis=1)
            acc_high = jnp.where(lane8 // 8 == 11 - j, rows, acc_high)
        beyond_low.append(acc_low)
        beyond_high.append(acc_high)
    mids = [jnp.concatenate(beyond_low, axis=0)] + [mine_at(i) for i in range(8)] + [jnp.concatenate(beyond_high, axis=0)]
    for g in range(GROUPS):
        qm[g, 4:36, :] = jnp.where(lane32 < 96, mids[g + 1], mids[g]) * KAPPA

    for item in across + corner:
        arrive(item)
    halos = [None] * 10
    for j, (block, lanes) in enumerate(((0, 96), (9, 64))):
        both = jnp.where(low8, yz_in[0, j], yz_in[1, j])
        parts = [pltpu.roll(both, (lanes - 32 * q) % 128, axis=1) for q in range(4)]
        halos[block] = jnp.concatenate(parts, axis=0)
    for m in range(4):
        left, right = pk_in[0, m], pk_in[1, m]
        halos[1 + m] = jnp.where(low32, left, pltpu.roll(right, 4, axis=1))
        halos[5 + m] = jnp.where(low32, pltpu.roll(left, 124, axis=1), right)
    for g in range(GROUPS):
        qh[g, 4:36, :] = jnp.where(lane32 < 96, halos[g + 1], halos[g]) * KAPPA
    for g in range(GROUPS):
        for i, first in enumerate((32, 4)):
            xe_out[i, g, 0:4, :] = qh[g, first : first + 4, :]
            xe_out[i, g, 4:8, :] = qm[g, first : first + 4, :]
    for item in ends:
        start(item)

    diag = iota((16, 128), 1) // 8 == 15 - iota((16, 128), 0)
    none = jnp.zeros((), BF16)

    def halo_planes(planes):
        left = []
        for x in planes:
            for g in range(GROUPS):
                field = jnp.broadcast_to(qh[g, pl.ds(x, 1), :], (16, 128))
                high = field.astype(BF16)
                rest = (field - high.astype(F32)).astype(BF16)
                left.append(jnp.concatenate([jnp.where(diag, high, none), jnp.where(diag, rest, none)], axis=1))
        left = jnp.concatenate(left, axis=0)
        spot = jnp.dot(left, spread, preferred_element_type=F32)
        for i, x in enumerate(planes):
            hal[x, 4:148, :] = spot[144 * i : 144 * i + 144]

    def edges(spans_d, spans_p, planes):
        def one(k, _):
            edge_pair(k, spans_d, spans_p)
            halo_planes(planes(k))
            return 0

        lax.fori_loop(0, PAIRS, one, 0)

    def edge_pair(k, spans_d, spans_p):
        a, b, c = off[k, 0], off[k, 1], off[k, 2]
        turn = lax.rem(128 + 8 * b - c, 128)
        step = jnp.where(b < 0, -1, 1)
        same = low == (slot - c < 4)
        for g in range(GROUPS):
            re[g + 1, 0:40, :] = pltpu.roll(jnp.where(same, qh[g], qm[g]), turn, axis=1)

        def lanes_of(n):
            lane_n = iota((n, 128), 1)
            return lane_n, lane_n % 8, 15 - lane_n // 8

        for first, n in spans_d:
            _, _, j_n = lanes_of(n)
            inner = jnp.logical_and(j_n + b >= 0, j_n + b < 16)
            for g in range(GROUPS):
                rows = pl.ds(a + first, n)
                diff = qh[g, first : first + n, :] - jnp.where(inner, re[g + 1, rows, :], re[g + 1 + step, rows, :])
                de[g, first : first + n, :] = diff * diff
        flag0 = jnp.where(c > 0, 5, 0)
        for first, n in spans_p:
            lane_n, slot_n, j_n = lanes_of(n)
            for g in range(GROUPS):
                field = de[g, first : first + n, :] + de[g, first + 1 : first + n + 1, :] + de[g, first + 2 : first + n + 2, :]
                fs[0, g + 1, first : first + n, :] = field
                fs[1, g + 1, first : first + n, :] = pltpu.roll(field, 8, axis=1)
                fs[2, g + 1, first : first + n, :] = pltpu.roll(field, 120, axis=1)
            x_at = gx * SX + iota((n, 128), 0) + (first - 3)
            is_to, is_at, is_one = slot_n == flag0, slot_n == flag0 + 1, slot_n == flag0 + 2
            x = x_at + jnp.where(is_to, a, 0)
            off_x = jnp.logical_or(is_one, jnp.logical_or(x < 0, x >= nx * SX))
            flag_x = jnp.where(off_x, 1.0, 0.0)
            is_flag = jnp.logical_and(slot_n >= flag0, slot_n < flag0 + 3)
            y_lane = gy * SY - 4 + j_n + jnp.where(is_to, b, 0)
            for g in range(GROUPS):
                rows = slice(first, first + n)
                up = jnp.where(lane_n >= 8, fs[1, g + 1, rows, :], fs[1, g + 2, rows, :])
                down = jnp.where(lane_n < 120, fs[2, g + 1, rows, :], fs[2, g, rows, :])
                field = fs[0, g + 1, rows, :] + up + down
                flag = flag_x
                if g in (0, GROUPS - 1):
                    y = y_lane + 16 * g
                    flag = jnp.where(jnp.logical_or(y < 0, y >= ny * SY), 1.0, flag_x)
                field = jnp.where(is_flag, flag, field)
                high = field.astype(BF16).astype(F32)
                eh[k, g, rows, :] = high
                el[k, g, rows, :] = field - high

    def inner_edges(k):
        edge_pair(k, [(0, 32)], [(0, 32)])

    def halo_eight(n, _):
        halo_planes([4 + 8 * n + i for i in range(8)])
        return 0

    inner_edges(jnp.int32(0))
    lax.fori_loop(0, 4, halo_eight, 0)


    def shifts(k):
        a, b, c = off[k, 0], off[k, 1], off[k, 2]
        turn = lax.rem(128 - c, 128)
        beyond = jnp.logical_or(lane8 < c, lane8 >= 128 + c)

        def square(x, t):
            rows = pl.ds(b + (8 * t + 4), 8)
            partner = pltpu.roll(jnp.where(beyond, hal[x + a, rows, :], sv[x + a, rows, :]), turn, axis=1)
            near[k, x, 8 * t : 8 * t + 8, :] = partner
            diff = sv[x, 8 * t + 4 : 8 * t + 12, :] - partner
            return diff * diff

        return square

    def begin(p, slot):
        def one(k, _):
            square = shifts(k)
            for t in range(17):
                d0, d1 = square(p, t), square(p + 1, t)
                carry[slot, k, 0, 8 * t : 8 * t + 8, :] = d0 + d1
                carry[slot, k, 1, 8 * t : 8 * t + 8, :] = d1
            return 0

        lax.fori_loop(0, PAIRS, one, 0)

    def field_step(k, n, slot, xs):
        p = n * BLOCK
        square = shifts(k)
        for t in range(17):
            rows = slice(8 * t, 8 * t + 8)
            d = [square(p + 2 + i, t) for i in range(BLOCK)]
            d01, d23, d45 = d[0] + d[1], d[2] + d[3], d[4] + d[5]
            sums = (carry[slot, k, 0, rows, :] + d[0], carry[slot, k, 1, rows, :] + d01, d01 + d[2], d[1] + d23, d23 + d[4], d[3] + d45)
            for i in range(BLOCK):
                xs[i, 8 + 8 * t : 16 + 8 * t, :] = sums[i]
            carry[slot, k, 0, rows, :] = d45
            carry[slot, k, 1, rows, :] = d[5]

    def weight_step(k, n, xs):
        p = n * BLOCK
        c = off[k, 2]
        beyond = jnp.logical_or(lane8 < 0 - c, lane8 >= 128 - c)
        turn = lax.rem(128 + c, 128)
        for i in range(0, BLOCK, TOGETHER):
            left = []
            for h in range(i, i + TOGETHER):
                for g in range(GROUPS):
                    r = 8 + 16 * g
                    field = xs[h, r - 1 : r + 15, :] + xs[h, r : r + 16, :] + xs[h, r + 1 : r + 17, :]
                    high = field.astype(BF16)
                    rest = (field - high.astype(F32)).astype(BF16)
                    e_high = jnp.broadcast_to(eh[k, g, pl.ds(p + h, 1), :], (16, 128)).astype(BF16)
                    e_rest = jnp.broadcast_to(el[k, g, pl.ds(p + h, 1), :], (16, 128)).astype(BF16)
                    left.append(
                        jnp.concatenate(
                            [high, rest, jnp.where(diag, e_high, none), jnp.where(diag, e_rest, none)], axis=1
                        )
                    )
            left = jnp.concatenate(left, axis=0)
            weight = jnp.exp2(jnp.dot(left, band[k], preferred_element_type=F32))
            for h in range(TOGETHER):
                w1[k, p + i + h] = weight[144 * h : 144 * h + 136, 0:128]
                w2[k, p + i + h] = weight[144 * h : 144 * h + 136, 128:256]
                for t in range(17):
                    rows, at = slice(8 * t, 8 * t + 8), slice(8 * t + 4, 8 * t + 12)
                    x = p + i + h + 1
                    back = pltpu.roll(jnp.where(beyond, hal[x, at, :], sv[x, at, :]), turn, axis=1)
                    t2[k, p + i + h, rows, :] = back * weight[144 * h + 8 * t : 144 * h + 8 * t + 8, 128:256]

    def run(steps, place, beside=None):
        def field(s, xs):
            k, n, slot = place(jnp.minimum(s, steps - 1))
            field_step(k, n, jnp.where(s < steps, slot, 2), xs)

        def weigh(s, xs):
            k, n, _ = place(s)
            weight_step(k, n, xs)

        field(jnp.int32(0), xa)

        def two_steps(i, _):
            s = 4 * i
            field(s + 1, xb)
            weigh(s, xa)
            field(s + 2, xa)
            weigh(s + 1, xb)
            field(s + 3, xb)
            weigh(s + 2, xa)
            field(s + 4, xa)
            weigh(s + 3, xb)
            if beside is not None:
                beside(i)
            return 0

        lax.fori_loop(0, steps // 4, two_steps, 0)

    begin(BLOCK, 0)
    run(PAIRS * 4, lambda s: (s // 4, 1 + s % 4, 0), lambda i: inner_edges(jnp.minimum(i + 1, PAIRS - 1)))

    for item in slabs + ends:
        arrive(item)
    for x in (0, 1, 2, 3, 36, 37, 38, 39):
        sv[x] = ext[x] * KAPPA
    for g in range(GROUPS):
        for i, first in enumerate((0, 36)):
            qh[g, first : first + 4, :] = xe_in[i, g, 0:4, :]
            qm[g, first : first + 4, :] = xe_in[i, g, 4:8, :]

    edges([(0, 16), (24, 16)], [(0, 8), (24, 16)], lambda k: [k, k + 36])
    begin(0, 1)
    run(PAIRS * 2, lambda s: (s // 2, 5 * (s % 2), 1 - s % 2))

    w2f, t2f = w2.reshape(PAIRS * 36 * 136, 128), t2.reshape(PAIRS * 36 * 136, 128)
    froms = [
        jnp.maximum((k * 36 + 3 - off[k, 0]) * 136 + 4 - off[k, 1], 1) for k in range(PAIRS)
    ]

    def finish(n, _):
        for x in (2 * n, 2 * n + 1):
            bases = [froms[k] + x * 136 for k in range(PAIRS)]
            for t in range(16):
                y = 8 * t
                num = sv[x + 4, y + 8 : y + 16, :]
                den = jnp.ones((8, 128), F32)
                for k in range(PAIRS):
                    rows = pl.ds(bases[k] + y, 8)
                    fore_w = w1[k, x + 3, y + 4 : y + 12, :]
                    num = num + (fore_w * near[k, x + 4, y + 4 : y + 12, :] + t2f[rows, :])
                    den = den + (fore_w + w2f[rows, :])
                done[x, y : y + 8, :] = num / (den * KAPPA)
            pltpu.make_async_copy(done.at[x], out.at[x], out_sem).start()
        return 0

    lax.fori_loop(0, SX // 2, finish, 0)
    pltpu.make_async_copy(done, out, out_sem).wait()
    for item in strips + across + corner + slabs + ends:
        leave(item)


PARTS = 4


def hand_over(src, dst, held, sems):
    n = SX // PARTS
    spans = [pl.ds(n * i, n) for i in range(PARTS)]
    ins = [pltpu.make_async_copy(src.at[span], held.at[span], sems.at[0, i]) for i, span in enumerate(spans)]
    outs = [pltpu.make_async_copy(held.at[span], dst.at[span], sems.at[1, i]) for i, span in enumerate(spans)]
    for item in ins:
        item.start()
    for first, then in zip(ins, outs):
        first.wait()
        then.start()
    for item in outs:
        item.wait()


def local(counts, volume, offsets):
    result = pl.pallas_call(
        functools.partial(kernel, counts),
        out_shape=jax.ShapeDtypeStruct((SX, SY, SZ), F32),
        in_specs=[pl.BlockSpec(memory_space=pltpu.SMEM), pl.BlockSpec(memory_space=pl.ANY)],
        out_specs=pl.BlockSpec(memory_space=pl.ANY),
        scratch_shapes=[
            pltpu.VMEM((40, 144, 128), F32),
            pltpu.VMEM((41, 144, 128), F32),
            pltpu.VMEM((41, 152, 128), F32),
            pltpu.VMEM((PAIRS, 38, 136, 128), F32),
            pltpu.VMEM((8 * 32, 128), F32),
            pltpu.VMEM((2, 4, 32, 128), F32),
            pltpu.VMEM((2, 4, 32, 128), F32),
            pltpu.VMEM((2, 8, 128), F32),
            pltpu.VMEM((2, 2, 8, 128), F32),
            pltpu.VMEM((2, GROUPS, 8, 128), F32),
            pltpu.VMEM((2, GROUPS, 8, 128), F32),
            pltpu.VMEM((GROUPS, 40, 128), F32),
            pltpu.VMEM((GROUPS, 40, 128), F32),
            pltpu.VMEM((GROUPS + 2, 48, 128), F32),
            pltpu.VMEM((GROUPS, 48, 128), F32),
            pltpu.VMEM((3, GROUPS + 2, 40, 128), F32),
            pltpu.VMEM((PAIRS, GROUPS, 40, 128), F32),
            pltpu.VMEM((PAIRS, GROUPS, 40, 128), F32),
            pltpu.VMEM((PAIRS, 512, 256), BF16),
            pltpu.VMEM((BLOCK, 168, 128), F32),
            pltpu.VMEM((BLOCK, 168, 128), F32),
            pltpu.VMEM((3, PAIRS, 2, 136, 128), F32),
            pltpu.VMEM((PAIRS, 36, 136, 128), F32),
            pltpu.VMEM((PAIRS, 36, 136, 128), F32),
            pltpu.VMEM((PAIRS, 36, 136, 128), F32),
            pltpu.VMEM((SX, SY, SZ), F32),
            pltpu.SemaphoreType.DMA((16,)),
            pltpu.SemaphoreType.DMA((16,)),
            pltpu.SemaphoreType.DMA((4,)),
            pltpu.SemaphoreType.DMA,
        ],
        compiler_params=pltpu.CompilerParams(
            collective_id=0, has_side_effects=True, vmem_limit_bytes=62 * 1024 * 1024
        ),
    )(offsets, volume)
    return pl.pallas_call(
        hand_over,
        out_shape=jax.ShapeDtypeStruct((SX, SY, SZ), F32),
        in_specs=[pl.BlockSpec(memory_space=pl.ANY)],
        out_specs=pl.BlockSpec(memory_space=pl.ANY),
        scratch_shapes=[pltpu.VMEM((SX, SY, SZ), F32), pltpu.SemaphoreType.DMA((2, PARTS))],
    )(result)


def solution(mesh):
    counts = (mesh.shape["gx"], mesh.shape["gy"], mesh.shape["gz"])
    spec = P("gx", "gy", "gz")
    return jax.shard_map(
        functools.partial(local, counts), mesh=mesh, in_specs=(spec, P()), out_specs=spec, check_vma=False
    )
```
